512 devices in a mesh: fsdp: 32 (over x, z_hi, core), replica: 16 (over y, z_lo).
Axes of the slice: x: 4, y: 8, z: 8 (z_hi: 4, z_lo: 2; z = z_hi * 2 + z_lo), core: 2. Of those that a mesh axis runs over, the one named last changes fastest.
Arguments:
- tokens: bfloat16 [16, 2048, 4096], P('replica', 'fsdp'), may hold values from -6 to 6
- cotangent: bfloat16 [16, 8192, 896], P('replica', 'fsdp'), may hold values from -0.29882812 to 0.29882812
- master: float32 [16, 4096, 896], P('replica', 'fsdp'), may hold values from -0.09375 to 0.09375
- moment_one: float32 [16, 4096, 896], P('replica', 'fsdp'), may hold values from -3 to 3
- moment_two: float32 [16, 4096, 896], P('replica', 'fsdp'), may hold values from 0.5 to 5
- anchor: float32 [4, 4, 32768], P(None, None, 'fsdp'), may hold values from -6 to 6
- outer_momentum: float32 [4, 4, 32768], P(None, None, 'fsdp'), may hold values from -3 to 3
- local_frag: bfloat16 [16, 4, 32768], P('replica', None, 'fsdp'), may hold values from -6 to 6
- frag_index: int32 [1], replicated, may hold values from 0 to 3
Outputs:
- new_master: float32 [16, 4096, 896], P('replica', 'fsdp')
- new_moment_one: float32 [16, 4096, 896], P('replica', 'fsdp')
- new_moment_two: float32 [16, 4096, 896], P('replica', 'fsdp')
- up_values: bfloat16 [16, 8192, 896], P('replica', 'fsdp')
- new_anchor: float32 [4, 32768], P(None, 'fsdp')
- new_momentum: float32 [4, 32768], P(None, 'fsdp')
The draws below stay inside these ranges and needn't reach their ends.
All inputs are finite; a program needn't handle non-finite values.
Results may differ from the reference program's by a relative error of at most 0.009.
Values may be sent and summed in bfloat16 or wider, within the bound.
A program may use at most 128 MiB of HBM per device.

```python
import math
import jax
import jax.numpy as jnp
from jax import lax

D = 4096
HGROUP = 4
TOK_DEV = 64
NFRAG = 4
HQ = 896
REPLICAS = 4
TOK_REP = 8192
TOK_SLAB = 2048
FRAG = 32768
N_FSDP = 32
N_REPLICA = 16


def block_levels(stream_key, shape, shards, least, top_value):
    def one(axis_at, blocks):
        heights = jax.random.uniform(jax.random.fold_in(jax.random.fold_in(stream_key, 6), axis_at), (blocks,), jnp.float32, least / len(shards), top_value / len(shards))
        return jnp.repeat(jnp.exp(heights), shape[axis_at] // blocks).reshape((-1,) + (1,) * (len(shape) - axis_at - 1))

    level = one(*shards[0])
    for cut in shards[1:]:
        level = level * one(*cut)
    return level


def scatter_about(key, shape, width, most, cuts=(), held_as=jnp.bfloat16):
    drawn = width * jax.random.normal(key, shape, jnp.float32)
    if cuts:
        drawn = drawn * block_levels(key, shape, cuts, -0.22, 0.18)
    return jnp.clip(drawn, -most, most).astype(held_as)


def setup_inputs(seed: int = 0) -> dict:
    streams_of = jax.random.split(jax.random.key(seed), 10)
    tokens = scatter_about(streams_of[0], (N_REPLICA, TOK_SLAB, D), 1.0, 6.0, ((0, 16), (1, 32)))
    cotangent = scatter_about(streams_of[1], (N_REPLICA, TOK_REP, HQ), 0.05, 0.29882812, ((0, 16), (1, 32)))
    master = scatter_about(streams_of[2], (N_REPLICA, D, HQ), D ** -0.5, 0.09375, ((0, 16), (1, 32)), jnp.float32)
    moment_one = scatter_about(streams_of[3], (N_REPLICA, D, HQ), 0.5, 3.0, ((0, 16), (1, 32)), jnp.float32)
    moment_two = jnp.clip(jnp.exp(math.log(5.0) - 2.3025851 * jax.random.uniform(streams_of[4], (N_REPLICA, D, HQ), jnp.float32) ** block_levels(streams_of[4], (N_REPLICA, D, HQ), ((0, 16), (1, 32)), -0.2, 0.2)), 0.5, 5.0)
    anchor = scatter_about(streams_of[5], (NFRAG, HGROUP, FRAG), 1.0, 6.0, ((2, 32),), jnp.float32)
    outer_momentum = scatter_about(streams_of[6], (NFRAG, HGROUP, FRAG), 0.5, 3.0, ((2, 32),), jnp.float32)
    local_frag = scatter_about(streams_of[7], (N_REPLICA, NFRAG, FRAG), 1.0, 6.0, ((0, 16), (2, 32)))
    frag_index = jax.random.randint(streams_of[8], (1,), 0, NFRAG).astype(jnp.int32)
    return dict(tokens=tokens, cotangent=cotangent, master=master, moment_one=moment_one, moment_two=moment_two, anchor=anchor, outer_momentum=outer_momentum, local_frag=local_frag, frag_index=frag_index)


beta_one = 0.9
beta_two = 0.95
adam_eps = 1e-08
inner_rate = 0.0003
decay_rate = 0.1
correct_one = 1.0 - 0.9 ** 20
correct_two = 1.0 - 0.95 ** 20
outer_rate = 0.7
outer_mu = 0.9

def adam_update(master, moment_one, moment_two, grad):
    new_one = beta_one * moment_one + (1.0 - beta_one) * grad
    new_two = beta_two * moment_two + (1.0 - beta_two) * grad * grad
    step_dir = new_one / correct_one / (jnp.sqrt(new_two / correct_two) + adam_eps)
    new_master = master - inner_rate * (step_dir + decay_rate * master)
    return (new_master, new_one, new_two)

def reference(tokens, cotangent, master, moment_one, moment_two, anchor, outer_momentum, local_frag, frag_index):
    grouped = tokens.reshape(REPLICAS, HGROUP, N_FSDP, TOK_DEV, D)
    grouped = jnp.transpose(grouped, (0, 2, 1, 3, 4)).reshape(REPLICAS, TOK_REP, D)

    def device_step(packed):
        index, upstream, weights_full, first_moment, second_moment = packed
        inputs = lax.dynamic_index_in_dim(grouped, index // HGROUP, 0, keepdims=False)
        weights = weights_full.astype(jnp.bfloat16)
        up_part = jnp.dot(inputs, weights, preferred_element_type=jnp.float32).astype(jnp.bfloat16)
        grad = jnp.dot(inputs.T, upstream, preferred_element_type=jnp.float32)
        new_master, new_one, new_two = adam_update(weights_full, first_moment, second_moment, grad)
        return (new_master, new_one, new_two, up_part)
    indices = jnp.arange(N_REPLICA, dtype=jnp.int32)
    new_master, new_one, new_two, up_values = lax.map(device_step, (indices, cotangent, master, moment_one, moment_two))
    fragment = frag_index[0].astype(jnp.int32)
    anchor_frag = lax.dynamic_index_in_dim(anchor, fragment, 0, keepdims=False)
    momentum_frag = lax.dynamic_index_in_dim(outer_momentum, fragment, 0, keepdims=False)
    local_sel = lax.dynamic_index_in_dim(local_frag, fragment, 1, keepdims=False).astype(jnp.float32)
    local_sel = local_sel.reshape(REPLICAS, HGROUP, FRAG)
    delta = lax.optimization_barrier(jnp.sum(anchor_frag[None] - local_sel, axis=0)) / REPLICAS
    new_momentum = outer_mu * momentum_frag + delta
    new_anchor = anchor_frag - outer_rate * (outer_mu * new_momentum + delta)
    return (new_master, new_one, new_two, up_values, new_anchor, new_momentum)
```

```python
import jax
import jax.numpy as jnp
from jax import lax
from jax.experimental import pallas as pl
from jax.experimental.pallas import tpu as pltpu
from jax.sharding import PartitionSpec as P

MESH = pl.DeviceIdType.MESH
F32 = jnp.float32
BF16 = jnp.bfloat16

beta_one = 0.9
beta_two = 0.95
adam_eps = 1e-08
inner_rate = 0.0003
decay_rate = 0.1
correct_one = 1.0 - 0.9**20
correct_two = 1.0 - 0.95**20
outer_rate = 0.7
outer_mu = 0.9

NX = 4
NZ = 4
QUARTERS = 4
TOK = 64
WIDE = 4096
COLS = WIDE // NX
HID = 896
ROWS = 128
TBLK = QUARTERS * TOK
N_COPIES = 64


def adam_update(master, moment_one, moment_two, grad):
    new_one = beta_one * moment_one + (1.0 - beta_one) * grad
    new_two = beta_two * moment_two + (1.0 - beta_two) * grad * grad
    step_dir = new_one / correct_one / (jnp.sqrt(new_two / correct_two) + adam_eps)
    new_master = master - inner_rate * (step_dir + decay_rate * master)
    return (new_master, new_one, new_two)


def nesterov(anchor_part, momentum_part, delta):
    new_momentum = outer_mu * momentum_part + delta
    new_anchor = anchor_part - outer_rate * (outer_mu * new_momentum + delta)
    return (new_anchor, new_momentum)


def mult(value, by):
    return pl.multiple_of(value, by)


def exchange(
    frag_ref,
    tok,
    cot,
    master,
    anchor,
    local_frag,
    grad_out,
    up_out,
    delta_out,
    tbuf,
    wbuf,
    cbuf,
    acc,
    upf,
    up_far,
    up_near,
    up_in,
    up_got,
    g_core,
    g_core_in,
    g_far,
    g_near,
    g_in,
    g_got,
    o_sum,
    o_in,
    ssem,
    rsem,
):
    fs = lax.axis_index("fsdp")
    rp = lax.axis_index("replica")
    x, zh, k = fs // 8, lax.rem(fs // 2, 4), lax.rem(fs, 2)
    y, zl = rp // 2, lax.rem(rp, 2)
    yl = lax.rem(y, 2)
    c = lax.rem(rp, 4)
    c_l = 2 * yl + (1 - zl)
    c_y = 2 * (1 - yl) + zl

    def at(dx=0, dz=0, core=k, yy=y, ll=zl):
        return (lax.rem(x + dx, 4) * 8 + lax.rem(zh + dz, 4) * 2 + core, yy * 2 + ll)

    def flip(bit):
        return y + bit * (1 - 2 * lax.rem(y // bit, 2))

    xp, x2, xm = at(1), at(2), at(3)
    zp, zm = at(0, 1), at(0, 3)
    co = at(core=1 - k)
    py, pl_ = at(yy=flip(1)), at(ll=1 - zl)
    y2, y4 = at(yy=flip(2)), at(yy=flip(4))

    barrier = pltpu.get_barrier_semaphore()
    partners = (xp, x2, xm, zp, zm, co, py, pl_, y2, y4)
    for partner in partners:
        pl.semaphore_signal(barrier, inc=1, device_id=partner, device_id_type=MESH)

    started = []

    def send(src, dst, to):
        number = len(started)
        copy = pltpu.make_async_remote_copy(
            src_ref=src,
            dst_ref=dst,
            send_sem=ssem.at[number],
            recv_sem=rsem.at[number],
            device_id=to,
            device_id_type=MESH,
        )
        copy.start()
        started.append(copy)
        return copy

    def trow(slot, quarter):
        return tbuf.at[pl.ds(mult(slot * TBLK + quarter * TOK, TOK), TOK), :]

    def piece(dx):
        return tok.at[0, :, pl.ds(mult(lax.rem(x + dx, 4) * COLS, COLS), COLS)]

    def woff(dz, core):
        return lax.rem(zh + dz, 4) * (2 * ROWS) + core * ROWS

    def whalf(dz, half):
        return wbuf.at[pl.ds(mult(woff(dz, k) + half * (ROWS // 2), ROWS // 2), ROWS // 2), :]

    def wfull(dz):
        return wbuf.at[pl.ds(mult(woff(dz, k), ROWS), ROWS), :]

    def chalf(slot, half):
        return cbuf.at[slot, pl.ds(half * (TBLK // 2), TBLK // 2), :]

    def own_chalf(half):
        return cot.at[0, pl.ds(half * (TBLK // 2), TBLK // 2), :]

    wbuf[pl.ds(mult(woff(0, k), ROWS), ROWS), :] = master[0].astype(BF16)
    tbuf[pl.ds(mult(c * TOK, TOK), TOK), :] = tok[0, :, pl.ds(mult(x * COLS, COLS), COLS)]

    frag = frag_ref[0]
    anchor_f = anchor[0]
    local_f = local_frag[0, 0:1, :].astype(F32)
    for i in range(1, 4):
        anchor_f = jnp.where(frag == i, anchor[i], anchor_f)
        local_f = jnp.where(frag == i, local_frag[0, i : i + 1, :].astype(F32), local_f)
    quarter = lax.broadcasted_iota(jnp.int32, anchor_f.shape, 0)
    o_sum[0] = jnp.where(quarter == c, anchor_f - local_f, 0.0)

    pl.semaphore_wait(barrier, len(partners))

    t_y = {}
    t_l = {}
    t_r = {}
    t_y[0] = send(trow(0, c), trow(0, c), py)
    t_l[0] = send(trow(0, c), trow(0, c), pl_)
    t_x2 = send(piece(2), trow(2, c), x2)
    t_xp = send(piece(1), trow(3, c), xp)
    t_xm = send(piece(3), trow(1, c), xm)
    w_pa = send(whalf(0, 0), whalf(0, 0), zp)
    w_mb = send(whalf(0, 1), whalf(0, 1), zm)
    c_pa = send(own_chalf(0), chalf(3, 0), xp)
    c_mb = send(own_chalf(1), chalf(1, 1), xm)
    w_pb = send(whalf(0, 1), whalf(0, 1), zp)
    w_ma = send(whalf(0, 0), whalf(0, 0), zm)
    c_pb = send(own_chalf(1), chalf(3, 1), xp)
    c_ma = send(own_chalf(0), chalf(1, 0), xm)
    w_co = [send(wfull(0), wfull(0), co)]
    o_copy = send(o_sum.at[0], o_in.at[0], y2)

    def outer_step(step, copy, to):
        copy.wait_recv()
        o_sum[step] = o_sum[step - 1] + o_in[step - 1]
        if to is None:
            return None
        return send(o_sum.at[step], o_in.at[step], to)

    for slot, copy in ((2, t_x2), (3, t_xp), (1, t_xm)):
        copy.wait_recv()
        t_l[slot] = send(trow(slot, c), trow(slot, c), pl_)
        t_y[slot] = send(trow(slot, c), trow(slot, c), py)

    t_l[0].wait_recv()
    t_r[0] = send(trow(0, c_l), trow(0, c_l), py)
    o_copy = outer_step(1, o_copy, y4)

    w_pa.wait_recv()
    w_ra = send(whalf(3, 0), whalf(3, 0), zp)
    w_mb.wait_recv()
    w_rb = send(whalf(1, 1), whalf(1, 1), zm)
    c_pa.wait_recv()
    c_ra = send(chalf(3, 0), chalf(2, 0), xp)
    c_mb.wait_recv()
    c_rb = send(chalf(1, 1), chalf(2, 1), xm)
    for slot in (2, 3, 1):
        t_l[slot].wait_recv()
        t_r[slot] = send(trow(slot, c_l), trow(slot, c_l), py)
    o_copy = outer_step(2, o_copy, pl_)
    w_pb.wait_recv()
    w_co.append(send(wfull(3), wfull(3), co))
    w_ma.wait_recv()
    w_co.append(send(wfull(1), wfull(1), co))
    o_copy = outer_step(3, o_copy, py)

    def add_grad(slot, first=False):
        part = cot.at[0] if slot == 0 else cbuf.at[slot]

        def tile(j, carry):
            cols = pl.ds(mult(j * 256, 256), 256)
            left = tbuf[slot * TBLK : (slot + 1) * TBLK, cols]
            prod = lax.dot_general(left, part[...], (((0,), (0,)), ((), ())), preferred_element_type=F32)
            if first:
                acc[cols, :] = prod
            else:
                acc[cols, :] += prod
            return carry

        lax.fori_loop(0, COLS // 256, tile, 0)

    def up_part(slot, store):
        left = slice(slot * TBLK, (slot + 1) * TBLK)
        for lo in range(0, HID, 256):
            hi = min(lo + 256, HID)
            store(lo, hi, jnp.dot(tbuf[left, :], wbuf[:, lo:hi], preferred_element_type=F32))

    def tokens_here(slot):
        t_y[slot].wait_recv()
        t_r[slot].wait_recv()

    tokens_here(0)
    add_grad(0, True)

    w_ra.wait_recv()
    w_co.append(send(whalf(2, 0), whalf(2, 0), co))
    w_rb.wait_recv()
    w_co.append(send(whalf(2, 1), whalf(2, 1), co))
    outer_step(4, o_copy, None)

    c_ra.wait_recv()
    c_rb.wait_recv()
    c_pb.wait_recv()
    c_ma.wait_recv()
    tokens_here(2)
    add_grad(2)
    for copy in w_co:
        copy.wait_recv()

    half_t = TBLK // 2
    half_r = ROWS // 2

    def store_far(lo, hi, value):
        up_far[:, lo:hi] = value.astype(BF16)

    def store_f(i):
        def store(lo, hi, value):
            upf[i, :, lo:hi] = value

        return store

    up_part(2, store_far)
    u_fp = send(up_far.at[pl.ds(0, half_t), :], up_in.at[0], xp)
    u_fm = send(up_far.at[pl.ds(half_t, half_t), :], up_in.at[1], xm)

    tokens_here(3)
    add_grad(3)
    tokens_here(1)
    add_grad(1)

    for e in (2, 1, 3, 0):
        rows = pl.ds(mult(woff(e, 1 - k), ROWS), ROWS)
        g_core[e] = acc[rows, :].astype(BF16)
        started_core = send(g_core.at[e], g_core_in.at[e], co)
        if e == 2:
            core_copies = {}
        core_copies[e] = started_core

    up_part(1, store_f(1))
    up_near[0, half_t:, :] = upf[1, half_t:, :].astype(BF16)
    u_pb = send(up_near.at[0, pl.ds(half_t, half_t), :], up_got.at[0, pl.ds(half_t, half_t), :], xp)
    up_part(3, store_f(2))
    up_near[1, :half_t, :] = upf[2, :half_t, :].astype(BF16)
    u_ma = send(up_near.at[1, pl.ds(0, half_t), :], up_got.at[1, pl.ds(0, half_t), :], xm)

    def core_sum(e):
        rows = pl.ds(mult(woff(e, k), ROWS), ROWS)
        core_copies[e].wait_recv()
        total = acc[rows, :] + g_core_in[e].astype(F32)
        acc[rows, :] = total
        return total

    g_far[...] = core_sum(2).astype(BF16)
    g_fp = send(g_far.at[pl.ds(0, half_r), :], g_in.at[0], zp)
    g_fm = send(g_far.at[pl.ds(half_r, half_r), :], g_in.at[1], zm)
    g_near[0] = core_sum(1).astype(BF16)
    g_pb = send(g_near.at[0, pl.ds(half_r, half_r), :], g_got.at[0, pl.ds(half_r, half_r), :], zp)
    g_near[1] = core_sum(3).astype(BF16)
    g_ma = send(g_near.at[1, pl.ds(0, half_r), :], g_got.at[1, pl.ds(0, half_r), :], zm)
    core_sum(0)
    up_part(0, store_f(0))

    u_fp.wait_recv()
    up_near[0, :half_t, :] = (upf[1, :half_t, :] + up_in[0].astype(F32)).astype(BF16)
    u_pa = send(up_near.at[0, pl.ds(0, half_t), :], up_got.at[0, pl.ds(0, half_t), :], xp)
    u_fm.wait_recv()
    up_near[1, half_t:, :] = (upf[2, half_t:, :] + up_in[1].astype(F32)).astype(BF16)
    u_mb = send(up_near.at[1, pl.ds(half_t, half_t), :], up_got.at[1, pl.ds(half_t, half_t), :], xm)

    def row_half(dz, half):
        return pl.ds(mult(woff(dz, k) + half * half_r, half_r), half_r)

    g_fp.wait_recv()
    g_near[0, :half_r, :] = (acc[row_half(1, 0), :] + g_in[0].astype(F32)).astype(BF16)
    g_pa = send(g_near.at[0, pl.ds(0, half_r), :], g_got.at[0, pl.ds(0, half_r), :], zp)
    g_fm.wait_recv()
    g_near[1, half_r:, :] = (acc[row_half(3, 1), :] + g_in[1].astype(F32)).astype(BF16)
    g_mb = send(g_near.at[1, pl.ds(half_r, half_r), :], g_got.at[1, pl.ds(half_r, half_r), :], zm)

    delta_out[...] = o_sum[4] * 0.25

    u_pb.wait_recv()
    u_ma.wait_recv()
    u_pa.wait_recv()
    u_mb.wait_recv()
    up_out[0] = (upf[0] + up_got[0].astype(F32) + up_got[1].astype(F32)).astype(BF16)
    g_pb.wait_recv()
    g_ma.wait_recv()
    g_pa.wait_recv()
    g_mb.wait_recv()
    own = pl.ds(mult(woff(0, k), ROWS), ROWS)
    grad_out[...] = acc[own, :] + g_got[0].astype(F32) + g_got[1].astype(F32)

    for copy in started:
        copy.wait_send()


def run_exchange(frag_index, tokens, cotangent, master, anchor, local_frag):
    vmem = pl.BlockSpec(memory_space=pltpu.VMEM)
    return pl.pallas_call(
        exchange,
        name="exchange",
        out_shape=(
            jax.ShapeDtypeStruct((ROWS, HID), F32),
            jax.ShapeDtypeStruct((1, TBLK, HID), BF16),
            jax.ShapeDtypeStruct((QUARTERS, 1024), F32),
        ),
        in_specs=[pl.BlockSpec(memory_space=pltpu.SMEM)] + [vmem] * 5,
        out_specs=(vmem, vmem, vmem),
        scratch_shapes=[
            pltpu.VMEM((NX * TBLK, COLS), BF16),
            pltpu.VMEM((COLS, HID), BF16),
            pltpu.VMEM((NX, TBLK, HID), BF16),
            pltpu.VMEM((COLS, HID), F32),
            pltpu.VMEM((3, TBLK, HID), F32),
            pltpu.VMEM((TBLK, HID), BF16),
            pltpu.VMEM((2, TBLK, HID), BF16),
            pltpu.VMEM((2, TBLK // 2, HID), BF16),
            pltpu.VMEM((2, TBLK, HID), BF16),
            pltpu.VMEM((4, ROWS, HID), BF16),
            pltpu.VMEM((4, ROWS, HID), BF16),
            pltpu.VMEM((ROWS, HID), BF16),
            pltpu.VMEM((2, ROWS, HID), BF16),
            pltpu.VMEM((2, ROWS // 2, HID), BF16),
            pltpu.VMEM((2, ROWS, HID), BF16),
            pltpu.VMEM((5, QUARTERS, 1024), F32),
            pltpu.VMEM((4, QUARTERS, 1024), F32),
            pltpu.SemaphoreType.DMA((N_COPIES,)),
            pltpu.SemaphoreType.DMA((N_COPIES,)),
        ],
        compiler_params=pltpu.CompilerParams(
            collective_id=0, has_side_effects=True, vmem_limit_bytes=48 * 2**20
        ),
    )(frag_index, tokens, cotangent, master, anchor, local_frag)


def local(
    tokens,
    cotangent,
    master,
    moment_one,
    moment_two,
    anchor,
    outer_momentum,
    local_frag,
    frag_index,
):
    grad, up_values, delta = run_exchange(frag_index, tokens, cotangent, master, anchor, local_frag)
    new_master, new_one, new_two = adam_update(master[0], moment_one[0], moment_two[0], grad)
    fragment = frag_index[0]
    anchor_frag = lax.dynamic_index_in_dim(anchor, fragment, 0, keepdims=False)
    momentum_frag = lax.dynamic_index_in_dim(outer_momentum, fragment, 0, keepdims=False)
    new_anchor, new_momentum = nesterov(anchor_frag, momentum_frag, delta)
    return (
        new_master[None],
        new_one[None],
        new_two[None],
        up_values,
        new_anchor,
        new_momentum,
    )


def solution(mesh):
    in_specs = (
        P("replica", "fsdp", None),
        P("replica", "fsdp", None),
        P("replica", "fsdp", None),
        P("replica", "fsdp", None),
        P("replica", "fsdp", None),
        P(None, None, "fsdp"),
        P(None, None, "fsdp"),
        P("replica", None, "fsdp"),
        P(),
    )
    out_specs = (
        P("replica", "fsdp", None),
        P("replica", "fsdp", None),
        P("replica", "fsdp", None),
        P("replica", "fsdp", None),
        P(None, "fsdp"),
        P(None, "fsdp"),
    )
    return jax.shard_map(local, mesh=mesh, in_specs=in_specs, out_specs=out_specs, check_vma=False)
```

```python
import jax
import jax.numpy as jnp
from jax import lax
from jax.experimental import pallas as pl
from jax.experimental.pallas import tpu as pltpu
from jax.sharding import PartitionSpec as P

MESH = pl.DeviceIdType.MESH
F32 = jnp.float32
BF16 = jnp.bfloat16

beta_one = 0.9
beta_two = 0.95
adam_eps = 1e-08
inner_rate = 0.0003
decay_rate = 0.1
correct_one = 1.0 - 0.9**20
correct_two = 1.0 - 0.95**20
outer_rate = 0.7
outer_mu = 0.9

NX = 4
NZ = 4
QUARTERS = 4
FRAGS = 4
TOK = 64
WIDE = 4096
COLS = WIDE // NX
HID = 896
ROWS = 128
TBLK = QUARTERS * TOK
N_COPIES = 64


def adam_decayed(master, moment_one, moment_two):
    return (master * (1.0 - inner_rate * decay_rate), beta_one * moment_one, beta_two * moment_two)


def adam_update(master, moment_one, moment_two, grad):
    new_one = moment_one + (1.0 - beta_one) * grad
    new_two = moment_two + (1.0 - beta_two) * (grad * grad)
    scale = jnp.sqrt(new_two * (1.0 / correct_two)) + adam_eps
    new_master = master - (inner_rate / correct_one) * (new_one / scale)
    return (new_master, new_one, new_two)


def nesterov(anchor_part, momentum_part, delta):
    new_momentum = outer_mu * momentum_part + delta
    new_anchor = anchor_part - outer_rate * (outer_mu * new_momentum + delta)
    return (new_anchor, new_momentum)


def mult(value, by):
    return pl.multiple_of(value, by)


class Sent:
    def __init__(self, copy):
        self.copy = copy
        self.here = False

    def wait_recv(self):
        if not self.here:
            self.here = True
            self.copy.wait_recv()


def exchange(
    tok,
    cot,
    master,
    local_hbm,
    one_hbm,
    two_hbm,
    master_out,
    one_out,
    two_out,
    up_out,
    sum_out,
    tbuf,
    wbuf,
    cbuf,
    acc,
    upf,
    up_far,
    up_near,
    up_in,
    up_got,
    g_core,
    g_core_in,
    g_far,
    g_near,
    g_in,
    g_got,
    o_part,
    o_in,
    o_all,
    master_v,
    one_v,
    two_v,
    local_frag,
    ssem,
    rsem,
    lsem,
):
    fs = lax.axis_index("fsdp")
    rp = lax.axis_index("replica")
    x, zh, k = fs // 8, lax.rem(fs // 2, 4), lax.rem(fs, 2)
    y, zl = rp // 2, lax.rem(rp, 2)
    yl = lax.rem(y, 2)
    c = lax.rem(rp, 4)
    c_l = 2 * yl + (1 - zl)

    def at(dx=0, dz=0, core=k, yy=y, ll=zl):
        return (lax.rem(x + dx, 4) * 8 + lax.rem(zh + dz, 4) * 2 + core, yy * 2 + ll)

    def flip(bit):
        return y + bit * (1 - 2 * lax.rem(y // bit, 2))

    xp, x2, xm = at(1), at(2), at(3)
    zp, zm = at(0, 1), at(0, 3)
    co = at(core=1 - k)
    py, pl_ = at(yy=flip(1)), at(ll=1 - zl)
    y2, y4 = at(yy=flip(2)), at(yy=flip(4))

    barrier = pltpu.get_barrier_semaphore()
    partners = (xp, x2, xm, zp, zm, co, py, pl_, y2, y4)
    for partner in partners:
        pl.semaphore_signal(barrier, inc=1, device_id=partner, device_id_type=MESH)

    started = []

    def send(src, dst, to):
        number = len(started)
        copy = pltpu.make_async_remote_copy(
            src_ref=src,
            dst_ref=dst,
            send_sem=ssem.at[number],
            recv_sem=rsem.at[number],
            device_id=to,
            device_id_type=MESH,
        )
        copy.start()
        started.append(Sent(copy))
        return started[-1]

    def trow(slot, quarter):
        return tbuf.at[pl.ds(mult(slot * TBLK + quarter * TOK, TOK), TOK), :]

    def piece(dx):
        return tok.at[0, :, pl.ds(mult(lax.rem(x + dx, 4) * COLS, COLS), COLS)]

    def woff(dz, core):
        return lax.rem(zh + dz, 4) * (2 * ROWS) + core * ROWS

    def whalf(dz, half):
        return wbuf.at[pl.ds(mult(woff(dz, k) + half * (ROWS // 2), ROWS // 2), ROWS // 2), :]

    def wfull(dz):
        return wbuf.at[pl.ds(mult(woff(dz, k), ROWS), ROWS), :]

    def chalf(slot, half):
        return cbuf.at[slot, pl.ds(half * (TBLK // 2), TBLK // 2), :]

    def own_chalf(half):
        return cot.at[0, pl.ds(half * (TBLK // 2), TBLK // 2), :]

    loads = [
        pltpu.make_async_copy(src, dst, lsem.at[i])
        for i, (src, dst) in enumerate(
            (
                (master.at[0], master_v),
                (piece(0), trow(0, c)),
                (local_hbm, local_frag),
                (cot.at[0], cbuf.at[0]),
                (one_hbm.at[0], one_v),
                (two_hbm.at[0], two_v),
            )
        )
    ]
    for load in loads:
        load.start()
    l_master, l_tok, l_local, l_cot, l_one, l_two = loads

    l_master.wait()
    wbuf[pl.ds(mult(woff(0, k), ROWS), ROWS), :] = master_v[...].astype(BF16)

    pl.semaphore_wait(barrier, len(partners))

    t_y, t_l, t_r = {}, {}, {}

    cp = {}

    def own_outer():
        for load in (l_tok, l_local, l_cot, l_one, l_two):
            load.wait()
        o_part[0] = local_frag[0].astype(F32)
        cp["o1"] = send(o_part.at[0], o_in.at[0], y2)

    def outer_two():
        cp["o1"].wait_recv()
        o_part[1] = o_part[0] + o_in[0]
        cp["o2"] = send(o_part.at[1], o_in.at[1], y4)

    def outer_three():
        cp["o2"].wait_recv()
        o_all[c] = o_part[1] + o_in[1]
        cp["o3"] = send(o_all.at[c], o_all.at[c], pl_)

    def outer_four():
        cp["o3"].wait_recv()
        o_two = pl.ds(2 * yl, 2)
        cp["o4"] = send(o_all.at[o_two], o_all.at[o_two], py)

    def put(name, src, dst, to):
        def step():
            cp[name] = send(src, dst, to)

        return step

    def after(name, *steps):
        def step():
            cp[name].wait_recv()
            for each in steps:
                each()

        return step

    def t_on(slot):
        def step():
            t_l[slot] = send(trow(slot, c), trow(slot, c), pl_)
            t_y[slot] = send(trow(slot, c), trow(slot, c), py)

        return step

    def t_relay(slot):
        def step():
            t_l[slot].wait_recv()
            t_r[slot] = send(trow(slot, c_l), trow(slot, c_l), py)

        return step

    def t_own():
        t_y[0] = send(piece(0), trow(0, c), py)
        t_l[0] = send(piece(0), trow(0, c), pl_)

    steps = {
        "t_own": t_own,
        "t_xp": put("t_xp", piece(1), trow(3, c), xp),
        "t_xm": put("t_xm", piece(3), trow(1, c), xm),
        "t_x2": put("t_x2", piece(2), trow(2, c), x2),
        "t_on3": after("t_xp", t_on(3)),
        "t_on1": after("t_xm", t_on(1)),
        "t_on2": after("t_x2", t_on(2)),
        "t_re0": t_relay(0),
        "t_re1": t_relay(1),
        "t_re2": t_relay(2),
        "t_re3": t_relay(3),
        "w_pa": put("w_pa", whalf(0, 0), whalf(0, 0), zp),
        "w_mb": put("w_mb", whalf(0, 1), whalf(0, 1), zm),
        "w_pb": put("w_pb", whalf(0, 1), whalf(0, 1), zp),
        "w_ma": put("w_ma", whalf(0, 0), whalf(0, 0), zm),
        "w_ra": after("w_pa", put("w_ra", whalf(3, 0), whalf(3, 0), zp)),
        "w_rb": after("w_mb", put("w_rb", whalf(1, 1), whalf(1, 1), zm)),
        "w_c0": put("w_c0", wfull(0), wfull(0), co),
        "w_c3": after("w_pb", put("w_c3", wfull(3), wfull(3), co)),
        "w_c1": after("w_ma", put("w_c1", wfull(1), wfull(1), co)),
        "w_c2a": after("w_ra", put("w_c2a", whalf(2, 0), whalf(2, 0), co)),
        "w_c2b": after("w_rb", put("w_c2b", whalf(2, 1), whalf(2, 1), co)),
        "c_pa": put("c_pa", own_chalf(0), chalf(3, 0), xp),
        "c_mb": put("c_mb", own_chalf(1), chalf(1, 1), xm),
        "c_pb": put("c_pb", own_chalf(1), chalf(3, 1), xp),
        "c_ma": put("c_ma", own_chalf(0), chalf(1, 0), xm),
        "c_ra": after("c_pa", put("c_ra", chalf(3, 0), chalf(2, 0), xp)),
        "c_rb": after("c_mb", put("c_rb", chalf(1, 1), chalf(2, 1), xm)),
        "o1": own_outer,
        "o2": outer_two,
        "o3": outer_three,
        "o4": outer_four,
    }
    order = (
        "t_own t_xp t_xm t_x2 w_pa w_mb w_c0 o1 t_on3 t_on1 c_pa c_mb t_re0 t_on2 c_pb c_ma w_pb w_ma o2 "
        "w_ra w_rb t_re3 c_ra c_rb t_re1 t_re2 o3 w_c3 w_c1 o4"
    )
    for step in order.split():
        steps[step]()

    def add_grad(slot, first=False):
        part = cbuf.at[slot]

        def tile(j, carry):
            cols = pl.ds(mult(j * 256, 256), 256)
            left = tbuf[slot * TBLK : (slot + 1) * TBLK, cols]
            prod = lax.dot_general(left, part[...], (((0,), (0,)), ((), ())), preferred_element_type=F32)
            if first:
                acc[cols, :] = prod
            else:
                acc[cols, :] += prod
            return carry

        lax.fori_loop(0, COLS // 256, tile, 0)

    def up_part(slot, store):
        left = slice(slot * TBLK, (slot + 1) * TBLK)
        for lo in range(0, HID, 256):
            hi = min(lo + 256, HID)
            store(lo, hi, jnp.dot(tbuf[left, :], wbuf[:, lo:hi], preferred_element_type=F32))

    def tokens_here(slot):
        t_y[slot].wait_recv()
        t_r[slot].wait_recv()

    half_t = TBLK // 2
    half_r = ROWS // 2
    tokens_here(0)
    add_grad(0, True)

    steps["w_c2a"]()
    steps["w_c2b"]()
    cp["o4"].wait_recv()
    sum_out[...] = o_all[...]
    master_v[...], one_v[...], two_v[...] = adam_decayed(master_v[...], one_v[...], two_v[...])

    for name in ("c_ra", "c_rb", "c_pb", "c_ma"):
        cp[name].wait_recv()
    tokens_here(2)
    add_grad(2)
    for name in ("w_c0", "w_c1", "w_c3", "w_c2a", "w_c2b"):
        cp[name].wait_recv()

    def store_far(lo, hi, value):
        up_far[:, lo:hi] = value.astype(BF16)

    def store_f(i):
        def store(lo, hi, value):
            upf[i, :, lo:hi] = value

        return store

    up_part(2, store_far)
    u_fp = send(up_far.at[pl.ds(0, half_t), :], up_in.at[0], xp)
    u_fm = send(up_far.at[pl.ds(half_t, half_t), :], up_in.at[1], xm)

    tokens_here(3)
    add_grad(3)
    up_part(3, store_f(2))
    up_near[1, :half_t, :] = upf[2, :half_t, :].astype(BF16)
    u_ma = send(up_near.at[1, pl.ds(0, half_t), :], up_got.at[1, pl.ds(0, half_t), :], xm)

    tokens_here(1)
    core_copies = {}
    for e in (2, 1, 3, 0):
        both = pl.ds(mult(woff(e, 0), 2 * ROWS), 2 * ROWS)
        left = tbuf[TBLK : 2 * TBLK, both]
        acc[both, :] += lax.dot_general(left, cbuf[1], (((0,), (0,)), ((), ())), preferred_element_type=F32)
        g_core[e] = acc[pl.ds(mult(woff(e, 1 - k), ROWS), ROWS), :].astype(BF16)
        core_copies[e] = send(g_core.at[e], g_core_in.at[e], co)

    def core_sum(e):
        rows = pl.ds(mult(woff(e, k), ROWS), ROWS)
        core_copies[e].wait_recv()
        total = acc[rows, :] + g_core_in[e].astype(F32)
        acc[rows, :] = total
        return total

    g_far[...] = core_sum(2).astype(BF16)
    g_fp = send(g_far.at[pl.ds(0, half_r), :], g_in.at[0], zp)
    g_fm = send(g_far.at[pl.ds(half_r, half_r), :], g_in.at[1], zm)
    g_near[0] = core_sum(1).astype(BF16)
    g_pb = send(g_near.at[0, pl.ds(half_r, half_r), :], g_got.at[0, pl.ds(half_r, half_r), :], zp)
    g_near[1] = core_sum(3).astype(BF16)
    g_ma = send(g_near.at[1, pl.ds(0, half_r), :], g_got.at[1, pl.ds(0, half_r), :], zm)
    core_sum(0)

    up_part(1, store_f(1))
    up_near[0, half_t:, :] = upf[1, half_t:, :].astype(BF16)
    u_pb = send(up_near.at[0, pl.ds(half_t, half_t), :], up_got.at[0, pl.ds(half_t, half_t), :], xp)

    u_fm.wait_recv()
    up_near[1, half_t:, :] = (upf[2, half_t:, :] + up_in[1].astype(F32)).astype(BF16)
    u_mb = send(up_near.at[1, pl.ds(half_t, half_t), :], up_got.at[1, pl.ds(half_t, half_t), :], xm)
    u_fp.wait_recv()
    up_near[0, :half_t, :] = (upf[1, :half_t, :] + up_in[0].astype(F32)).astype(BF16)
    u_pa = send(up_near.at[0, pl.ds(0, half_t), :], up_got.at[0, pl.ds(0, half_t), :], xp)
    up_part(0, store_f(0))

    def row_half(dz, half):
        return pl.ds(mult(woff(dz, k) + half * half_r, half_r), half_r)

    g_fp.wait_recv()
    g_near[0, :half_r, :] = (acc[row_half(1, 0), :] + g_in[0].astype(F32)).astype(BF16)
    g_pa = send(g_near.at[0, pl.ds(0, half_r), :], g_got.at[0, pl.ds(0, half_r), :], zp)
    g_fm.wait_recv()
    g_near[1, half_r:, :] = (acc[row_half(3, 1), :] + g_in[1].astype(F32)).astype(BF16)
    g_mb = send(g_near.at[1, pl.ds(half_r, half_r), :], g_got.at[1, pl.ds(half_r, half_r), :], zm)

    for copy in (u_pb, u_ma, u_pa, u_mb):
        copy.wait_recv()
    up_out[0] = (upf[0] + up_got[0].astype(F32) + up_got[1].astype(F32)).astype(BF16)
    for copy in (g_pb, g_ma, g_pa, g_mb):
        copy.wait_recv()
    own = pl.ds(mult(woff(0, k), ROWS), ROWS)
    grad = acc[own, :] + g_got[0].astype(F32) + g_got[1].astype(F32)
    master_out[0], one_out[0], two_out[0] = adam_update(master_v[...], one_v[...], two_v[...], grad)

    for sent in started:
        sent.copy.wait_send()


STATE = jax.ShapeDtypeStruct((1, ROWS, HID), F32)
RESULTS = (
    STATE,
    STATE,
    STATE,
    jax.ShapeDtypeStruct((1, TBLK, HID), BF16),
)
SLICES = (FRAGS, 1024)


def run_exchange(*operands):
    vmem = pl.BlockSpec(memory_space=pltpu.VMEM)
    return pl.pallas_call(
        exchange,
        name="exchange",
        out_shape=RESULTS + (jax.ShapeDtypeStruct((QUARTERS,) + SLICES, F32),),
        in_specs=[pl.BlockSpec(memory_space=pl.ANY)] * 6,
        out_specs=(vmem,) * 5,
        scratch_shapes=[
            pltpu.VMEM((NX * TBLK, COLS), BF16),
            pltpu.VMEM((COLS, HID), BF16),
            pltpu.VMEM((NX, TBLK, HID), BF16),
            pltpu.VMEM((COLS, HID), F32),
            pltpu.VMEM((3, TBLK, HID), F32),
            pltpu.VMEM((TBLK, HID), BF16),
            pltpu.VMEM((2, TBLK, HID), BF16),
            pltpu.VMEM((2, TBLK // 2, HID), BF16),
            pltpu.VMEM((2, TBLK, HID), BF16),
            pltpu.VMEM((4, ROWS, HID), BF16),
            pltpu.VMEM((4, ROWS, HID), BF16),
            pltpu.VMEM((ROWS, HID), BF16),
            pltpu.VMEM((2, ROWS, HID), BF16),
            pltpu.VMEM((2, ROWS // 2, HID), BF16),
            pltpu.VMEM((2, ROWS, HID), BF16),
            pltpu.VMEM((2,) + SLICES, F32),
            pltpu.VMEM((2,) + SLICES, F32),
            pltpu.VMEM((QUARTERS,) + SLICES, F32),
            pltpu.VMEM((ROWS, HID), F32),
            pltpu.VMEM((ROWS, HID), F32),
            pltpu.VMEM((ROWS, HID), F32),
            pltpu.VMEM((1,) + SLICES, BF16),
            pltpu.SemaphoreType.DMA((N_COPIES,)),
            pltpu.SemaphoreType.DMA((N_COPIES,)),
            pltpu.SemaphoreType.DMA((6,)),
        ],
        compiler_params=pltpu.CompilerParams(
            collective_id=0, has_side_effects=True, vmem_limit_bytes=int(51.85 * 2**20)
        ),
    )(*operands)


def finish(frag_ref, sums, anchor, momentum, master, one, two, up, master_o, one_o, two_o, up_o, anchor_o, momentum_o, buf, sem):
    pairs = ((master, master_o), (one, one_o), (two, two_o), (up, up_o))
    copies = [pltpu.make_async_copy(src, dst, sem.at[i]) for i, (src, dst) in enumerate(pairs)]
    for copy in copies:
        copy.start()
    frag = frag_ref[0]
    for quarter in range(QUARTERS):
        row = slice(quarter, quarter + 1)
        local_sum = sums[quarter, 0:1, :]
        anchor_f = anchor[0, row, :]
        momentum_f = momentum[0, row, :]
        for i in range(1, FRAGS):
            local_sum = jnp.where(frag == i, sums[quarter, i : i + 1, :], local_sum)
            anchor_f = jnp.where(frag == i, anchor[i, row, :], anchor_f)
            momentum_f = jnp.where(frag == i, momentum[i, row, :], momentum_f)
        buf[0, row, :], buf[1, row, :] = nesterov(anchor_f, momentum_f, anchor_f - local_sum * 0.25)
    for i, out in enumerate((anchor_o, momentum_o)):
        copies.append(pltpu.make_async_copy(buf.at[i], out, sem.at[4 + i]))
        copies[-1].start()
    for copy in copies:
        copy.wait()


def run_finish(*given):
    place = pl.BlockSpec(memory_space=pl.ANY)
    vmem = pl.BlockSpec(memory_space=pltpu.VMEM)
    small = jax.ShapeDtypeStruct((QUARTERS, 1024), F32)
    return pl.pallas_call(
        finish,
        name="finish",
        out_shape=RESULTS + (small, small),
        in_specs=[pl.BlockSpec(memory_space=pltpu.SMEM)] + [vmem] * 3 + [place] * 4,
        out_specs=(place,) * 6,
        scratch_shapes=[pltpu.VMEM((2, QUARTERS, 1024), F32), pltpu.SemaphoreType.DMA((6,))],
        compiler_params=pltpu.CompilerParams(vmem_limit_bytes=2**20),
    )(*given)


def local(
    tokens,
    cotangent,
    master,
    moment_one,
    moment_two,
    anchor,
    outer_momentum,
    local_frag,
    frag_index,
):
    *results, sums = run_exchange(tokens, cotangent, master, local_frag, moment_one, moment_two)
    return run_finish(frag_index, sums, anchor, outer_momentum, *results)


def solution(mesh):
    in_specs = (
        P("replica", "fsdp", None),
        P("replica", "fsdp", None),
        P("replica", "fsdp", None),
        P("replica", "fsdp", None),
        P("replica", "fsdp", None),
        P(None, None, "fsdp"),
        P(None, None, "fsdp"),
        P("replica", None, "fsdp"),
        P(),
    )
    out_specs = (
        P("replica", "fsdp", None),
        P("replica", "fsdp", None),
        P("replica", "fsdp", None),
        P("replica", "fsdp", None),
        P(None, "fsdp"),
        P(None, "fsdp"),
    )
    return jax.shard_map(local, mesh=mesh, in_specs=in_specs, out_specs=out_specs, check_vma=False)
```

```python
import jax
import jax.numpy as jnp
from jax import lax
from jax.experimental import pallas as pl
from jax.experimental.pallas import tpu as pltpu
from jax.sharding import PartitionSpec as P

MESH = pl.DeviceIdType.MESH
F32 = jnp.float32
BF16 = jnp.bfloat16

beta_one = 0.9
beta_two = 0.95
adam_eps = 1e-08
inner_rate = 0.0003
decay_rate = 0.1
correct_one = 1.0 - 0.9**20
correct_two = 1.0 - 0.95**20
outer_rate = 0.7
outer_mu = 0.9

NX = 4
NZ = 4
QUARTERS = 4
FRAGS = 4
TOK = 64
WIDE = 4096
COLS = WIDE // NX
HALF = COLS // 2
HID = 896
ROWS = 128
TBLK = QUARTERS * TOK
N_COPIES = 80


def adam_decayed(master, moment_one, moment_two):
    return (master * (1.0 - inner_rate * decay_rate), beta_one * moment_one, beta_two * moment_two)


def adam_update(master, moment_one, moment_two, grad):
    new_one = moment_one + (1.0 - beta_one) * grad
    new_two = moment_two + (1.0 - beta_two) * (grad * grad)
    scale = jnp.sqrt(new_two * (1.0 / correct_two)) + adam_eps
    new_master = master - (inner_rate / correct_one) * (new_one / scale)
    return (new_master, new_one, new_two)


def nesterov(anchor_part, momentum_part, delta):
    new_momentum = outer_mu * momentum_part + delta
    new_anchor = anchor_part - outer_rate * (outer_mu * new_momentum + delta)
    return (new_anchor, new_momentum)


def mult(value, by):
    return pl.multiple_of(value, by)


ORDER_ONE = ("t0_own t0_xp t0_xm t0_x2 w_pa w_mb w_c0 t1_own c_pa c_mb t0_on3 t0_on1 t0_on2 o1 t1_xp t1_xm t1_x2 t0_re0 c_pb c_ma t0_re3 t0_re1 t0_re2 t1_on3 t1_on1 t1_on2 o2 w_ra w_rb t1_re0 c_ra c_rb t1_re3 w_pb w_ma t1_re1 t1_re2 o3",)
ORDER_TWO = ("w_c3 w_c1",)
ORDER_THREE = ("o4 w_c2a w_c2b",)


class Sent:
    def __init__(self, copy):
        self.copy = copy
        self.here = False

    def wait_recv(self):
        if not self.here:
            self.here = True
            self.copy.wait_recv()


def exchange(
    tok,
    cot,
    master,
    local_hbm,
    one_hbm,
    two_hbm,
    master_out,
    one_out,
    two_out,
    up_out,
    sum_out,
    tbuf,
    wbuf,
    cbuf,
    acc,
    upf,
    up_far,
    up_near,
    up_in,
    up_got,
    g_core,
    g_core_in,
    g_far,
    g_near,
    g_in,
    g_got,
    o_part,
    o_in,
    o_all,
    master_v,
    one_v,
    two_v,
    local_frag,
    ssem,
    rsem,
    lsem,
):
    fs = lax.axis_index("fsdp")
    rp = lax.axis_index("replica")
    x, zh, k = fs // 8, lax.rem(fs // 2, 4), lax.rem(fs, 2)
    y, zl = rp // 2, lax.rem(rp, 2)
    yl = lax.rem(y, 2)
    c = lax.rem(rp, 4)
    c_l = 2 * yl + (1 - zl)

    def at(dx=0, dz=0, core=k, yy=y, ll=zl):
        return (lax.rem(x + dx, 4) * 8 + lax.rem(zh + dz, 4) * 2 + core, yy * 2 + ll)

    def flip(bit):
        return y + bit * (1 - 2 * lax.rem(y // bit, 2))

    xp, x2, xm = at(1), at(2), at(3)
    zp, zm = at(0, 1), at(0, 3)
    co = at(core=1 - k)
    py, pl_ = at(yy=flip(1)), at(ll=1 - zl)
    y2, y4 = at(yy=flip(2)), at(yy=flip(4))

    barrier = pltpu.get_barrier_semaphore()
    partners = (xp, x2, xm, zp, zm, co, py, pl_, y2, y4)
    for partner in partners:
        pl.semaphore_signal(barrier, inc=1, device_id=partner, device_id_type=MESH)

    started = []

    def send(src, dst, to):
        number = len(started)
        copy = pltpu.make_async_remote_copy(
            src_ref=src,
            dst_ref=dst,
            send_sem=ssem.at[number],
            recv_sem=rsem.at[number],
            device_id=to,
            device_id_type=MESH,
        )
        copy.start()
        started.append(Sent(copy))
        return started[-1]

    own_pair = zh // 2
    pairs = (1 - own_pair, own_pair)

    def trow(rnd, slot, quarter):
        return tbuf.at[rnd, pl.ds(mult(slot * TBLK + quarter * TOK, TOK), TOK), :]

    def piece(rnd, dx):
        return tok.at[0, :, pl.ds(mult(lax.rem(x + dx, 4) * COLS + pairs[rnd] * HALF, HALF), HALF)]

    def woff(dz, core):
        return lax.rem(zh + dz, 4) * (2 * ROWS) + core * ROWS

    def whalf(dz, half):
        return wbuf.at[pl.ds(mult(woff(dz, k) + half * (ROWS // 2), ROWS // 2), ROWS // 2), :]

    def wfull(dz):
        return wbuf.at[pl.ds(mult(woff(dz, k), ROWS), ROWS), :]

    def chalf(slot, half):
        return cbuf.at[pl.ds(slot * TBLK + half * (TBLK // 2), TBLK // 2), :]

    def own_chalf(half):
        return cot.at[0, pl.ds(half * (TBLK // 2), TBLK // 2), :]

    loads = [
        pltpu.make_async_copy(src, dst, lsem.at[i])
        for i, (src, dst) in enumerate(
            (
                (master.at[0], master_v),
                (piece(0, 0), trow(0, 0, c)),
                (piece(1, 0), trow(1, 0, c)),
                (local_hbm, local_frag),
                (cot.at[0], cbuf.at[pl.ds(0, TBLK), :]),
                (one_hbm.at[0], one_v),
                (two_hbm.at[0], two_v),
            )
        )
    ]
    for load in loads:
        load.start()
    l_master, l_tok, l_tok2, l_local, l_cot, l_one, l_two = loads

    l_master.wait()
    wbuf[pl.ds(mult(woff(0, k), ROWS), ROWS), :] = master_v[...].astype(BF16)

    pl.semaphore_wait(barrier, len(partners))

    t_y, t_l, t_r = {}, {}, {}

    cp = {}

    def own_outer():
        for load in (l_tok, l_tok2, l_local, l_cot, l_one, l_two):
            load.wait()
        o_part[0] = local_frag[0].astype(F32)
        cp["o1"] = send(o_part.at[0], o_in.at[0], y2)

    def outer_two():
        cp["o1"].wait_recv()
        o_part[1] = o_part[0] + o_in[0]
        cp["o2"] = send(o_part.at[1], o_in.at[1], y4)

    def outer_three():
        cp["o2"].wait_recv()
        o_all[c] = o_part[1] + o_in[1]
        cp["o3"] = send(o_all.at[c], o_all.at[c], pl_)

    def outer_four():
        cp["o3"].wait_recv()
        o_two = pl.ds(2 * yl, 2)
        cp["o4"] = send(o_all.at[o_two], o_all.at[o_two], py)

    def put(name, src, dst, to):
        def step():
            cp[name] = send(src, dst, to)

        return step

    def after(name, *steps):
        def step():
            cp[name].wait_recv()
            for each in steps:
                each()

        return step

    def t_on(rnd, slot):
        def step():
            t_l[rnd, slot] = send(trow(rnd, slot, c), trow(rnd, slot, c), pl_)
            t_y[rnd, slot] = send(trow(rnd, slot, c), trow(rnd, slot, c), py)

        return step

    def t_relay(rnd, slot):
        def step():
            t_l[rnd, slot].wait_recv()
            t_r[rnd, slot] = send(trow(rnd, slot, c_l), trow(rnd, slot, c_l), py)

        return step

    def t_own(rnd):
        def step():
            t_y[rnd, 0] = send(piece(rnd, 0), trow(rnd, 0, c), py)
            t_l[rnd, 0] = send(piece(rnd, 0), trow(rnd, 0, c), pl_)

        return step

    steps = {
        "w_pa": put("w_pa", whalf(0, 0), whalf(0, 0), zp),
        "w_mb": put("w_mb", whalf(0, 1), whalf(0, 1), zm),
        "w_pb": put("w_pb", whalf(0, 1), whalf(0, 1), zp),
        "w_ma": put("w_ma", whalf(0, 0), whalf(0, 0), zm),
        "w_ra": after("w_pa", put("w_ra", whalf(3, 0), whalf(3, 0), zp)),
        "w_rb": after("w_mb", put("w_rb", whalf(1, 1), whalf(1, 1), zm)),
        "w_c0": put("w_c0", wfull(0), wfull(0), co),
        "w_c3": after("w_pb", put("w_c3", wfull(3), wfull(3), co)),
        "w_c1": after("w_ma", put("w_c1", wfull(1), wfull(1), co)),
        "w_c2a": after("w_ra", put("w_c2a", whalf(2, 0), whalf(2, 0), co)),
        "w_c2b": after("w_rb", put("w_c2b", whalf(2, 1), whalf(2, 1), co)),
        "c_pa": put("c_pa", own_chalf(0), chalf(3, 0), xp),
        "c_mb": put("c_mb", own_chalf(1), chalf(1, 1), xm),
        "c_pb": put("c_pb", own_chalf(1), chalf(3, 1), xp),
        "c_ma": put("c_ma", own_chalf(0), chalf(1, 0), xm),
        "c_ra": after("c_pa", put("c_ra", chalf(3, 0), chalf(2, 0), xp)),
        "c_rb": after("c_mb", put("c_rb", chalf(1, 1), chalf(2, 1), xm)),
        "o1": own_outer,
        "o2": outer_two,
        "o3": outer_three,
        "o4": outer_four,
    }
    for r in range(2):
        steps[f"t{r}_own"] = t_own(r)
        for slot, name, to in ((3, "xp", xp), (1, "xm", xm), (2, "x2", x2)):
            steps[f"t{r}_{name}"] = put(f"t{r}_{name}", piece(r, 4 - slot), trow(r, slot, c), to)
            steps[f"t{r}_on{slot}"] = after(f"t{r}_{name}", t_on(r, slot))
        for slot in range(NX):
            steps[f"t{r}_re{slot}"] = t_relay(r, slot)

    def run(order):
        for step in " ".join(order).split():
            steps[step]()

    run(ORDER_ONE)

    half_t = TBLK // 2
    half_r = ROWS // 2
    odd = lax.rem(zh, 2)
    far = lax.rem(zh + 2, 4)
    blocks = (far, 3 - zh, zh + 1 - 2 * odd, zh)
    core_copies = []

    def tokens_here(rnd, slot):
        t_y[rnd, slot].wait_recv()
        t_r[rnd, slot].wait_recv()

    def grad_part(i, lo, hi):
        rnd = i // 2
        col = pl.ds(mult(lax.rem(blocks[i], 2) * 256, 256), 256)
        left = tbuf[rnd, lo * TBLK : hi * TBLK, col]
        right = cbuf[lo * TBLK : hi * TBLK, :]
        return lax.dot_general(left, right, (((0,), (0,)), ((), ())), preferred_element_type=F32)

    def both_rows(i):
        return pl.ds(mult(blocks[i] * 2 * ROWS, 2 * ROWS), 2 * ROWS)

    def rows_of(i, core):
        return pl.ds(mult(blocks[i] * 2 * ROWS + core * ROWS, ROWS), ROWS)

    def core_send(i):
        g_core[i] = acc[rows_of(i, 1 - k), :].astype(BF16)
        core_copies.append(send(g_core.at[i], g_core_in.at[i], co))

    def core_sum(i):
        core_copies[i].wait_recv()
        total = acc[rows_of(i, k), :] + g_core_in[i].astype(F32)
        acc[rows_of(i, k), :] = total
        return total

    def up_part(slot, store):
        rows = slice(slot * TBLK, (slot + 1) * TBLK)
        for lo in range(0, HID, 256):
            hi = min(lo + 256, HID)
            total = None
            for rnd in range(2):
                weights = wbuf[pl.ds(mult(pairs[rnd] * HALF, HALF), HALF), lo:hi]
                part = jnp.dot(tbuf[rnd, rows, :], weights, preferred_element_type=F32)
                total = part if total is None else total + part
            store(lo, hi, total)

    for name in ("c_ra", "c_rb", "c_pb", "c_ma"):
        cp[name].wait_recv()
    for slot in range(NX):
        tokens_here(0, slot)
    for i in (0, 1):
        acc[both_rows(i), :] = grad_part(i, 0, NX)
        core_send(i)
    run(ORDER_TWO)
    g_far[...] = core_sum(0).astype(BF16)
    g_fp = send(g_far.at[pl.ds(0, half_r), :], g_in.at[0], zp)
    g_fm = send(g_far.at[pl.ds(half_r, half_r), :], g_in.at[1], zm)
    core_sum(1)
    run(ORDER_THREE)

    def store_far(lo, hi, value):
        up_far[:, lo:hi] = value.astype(BF16)

    def store_f(i):
        def store(lo, hi, value):
            upf[i, :, lo:hi] = value

        return store

    master_v[...], one_v[...], two_v[...] = adam_decayed(master_v[...], one_v[...], two_v[...])
    for name in ("w_c0", "w_c1", "w_c3", "w_c2a", "w_c2b"):
        cp[name].wait_recv()
    tokens_here(1, 2)
    up_part(2, store_far)
    u_fp = send(up_far.at[pl.ds(0, half_t), :], up_in.at[0], xp)
    u_fm = send(up_far.at[pl.ds(half_t, half_t), :], up_in.at[1], xm)

    tokens_here(1, 0)
    tokens_here(1, 1)
    tokens_here(1, 3)
    for i in (2, 3):
        acc[both_rows(i), :] = grad_part(i, 0, NX)
        core_send(i)

    up_part(3, store_f(2))
    up_near[1, :half_t, :] = upf[2, :half_t, :].astype(BF16)
    u_ma = send(up_near.at[1, pl.ds(0, half_t), :], up_got.at[1, pl.ds(0, half_t), :], xm)

    core_sum(2)
    near = [pl.ds(mult(woff(e, k), ROWS), ROWS) for e in (1, 3)]
    g_near[0] = acc[near[0], :].astype(BF16)
    g_pb = send(g_near.at[0, pl.ds(half_r, half_r), :], g_got.at[0, pl.ds(half_r, half_r), :], zp)
    g_near[1] = acc[near[1], :].astype(BF16)
    g_ma = send(g_near.at[1, pl.ds(0, half_r), :], g_got.at[1, pl.ds(0, half_r), :], zm)

    up_part(1, store_f(1))
    up_near[0, half_t:, :] = upf[1, half_t:, :].astype(BF16)
    u_pb = send(up_near.at[0, pl.ds(half_t, half_t), :], up_got.at[0, pl.ds(half_t, half_t), :], xp)
    def row_half(dz, half):
        return pl.ds(mult(woff(dz, k) + half * half_r, half_r), half_r)

    g_fp.wait_recv()
    g_near[0, :half_r, :] = (acc[row_half(1, 0), :] + g_in[0].astype(F32)).astype(BF16)
    g_pa = send(g_near.at[0, pl.ds(0, half_r), :], g_got.at[0, pl.ds(0, half_r), :], zp)
    g_fm.wait_recv()
    g_near[1, half_r:, :] = (acc[row_half(3, 1), :] + g_in[1].astype(F32)).astype(BF16)
    g_mb = send(g_near.at[1, pl.ds(half_r, half_r), :], g_got.at[1, pl.ds(half_r, half_r), :], zm)

    u_fm.wait_recv()
    up_near[1, half_t:, :] = (upf[2, half_t:, :] + up_in[1].astype(F32)).astype(BF16)
    u_mb = send(up_near.at[1, pl.ds(half_t, half_t), :], up_got.at[1, pl.ds(half_t, half_t), :], xm)
    u_fp.wait_recv()
    up_near[0, :half_t, :] = (upf[1, :half_t, :] + up_in[0].astype(F32)).astype(BF16)
    u_pa = send(up_near.at[0, pl.ds(0, half_t), :], up_got.at[0, pl.ds(0, half_t), :], xp)
    up_part(0, store_f(0))
    core_sum(3)
    cp["o4"].wait_recv()
    sum_out[...] = o_all[...]

    for copy in (u_pb, u_ma, u_pa, u_mb):
        copy.wait_recv()
    up_out[0] = (upf[0] + up_got[0].astype(F32) + up_got[1].astype(F32)).astype(BF16)
    for copy in (g_pb, g_ma, g_pa, g_mb):
        copy.wait_recv()
    own = pl.ds(mult(woff(0, k), ROWS), ROWS)
    grad = acc[own, :] + g_got[0].astype(F32) + g_got[1].astype(F32)
    master_out[0], one_out[0], two_out[0] = adam_update(master_v[...], one_v[...], two_v[...], grad)

    for sent in started:
        sent.copy.wait_send()


STATE = jax.ShapeDtypeStruct((1, ROWS, HID), F32)
RESULTS = (
    STATE,
    STATE,
    STATE,
    jax.ShapeDtypeStruct((1, TBLK, HID), BF16),
)
SLICES = (FRAGS, 1024)


def run_exchange(*operands):
    vmem = pl.BlockSpec(memory_space=pltpu.VMEM)
    return pl.pallas_call(
        exchange,
        name="exchange",
        out_shape=RESULTS + (jax.ShapeDtypeStruct((QUARTERS,) + SLICES, F32),),
        in_specs=[pl.BlockSpec(memory_space=pl.ANY)] * 6,
        out_specs=(vmem,) * 5,
        scratch_shapes=[
            pltpu.VMEM((2, NX * TBLK, HALF), BF16),
            pltpu.VMEM((COLS, HID), BF16),
            pltpu.VMEM((NX * TBLK, HID), BF16),
            pltpu.VMEM((COLS, HID), F32),
            pltpu.VMEM((3, TBLK, HID), F32),
            pltpu.VMEM((TBLK, HID), BF16),
            pltpu.VMEM((2, TBLK, HID), BF16),
            pltpu.VMEM((2, TBLK // 2, HID), BF16),
            pltpu.VMEM((2, TBLK, HID), BF16),
            pltpu.VMEM((4, ROWS, HID), BF16),
            pltpu.VMEM((4, ROWS, HID), BF16),
            pltpu.VMEM((ROWS, HID), BF16),
            pltpu.VMEM((2, ROWS, HID), BF16),
            pltpu.VMEM((2, ROWS // 2, HID), BF16),
            pltpu.VMEM((2, ROWS, HID), BF16),
            pltpu.VMEM((2,) + SLICES, F32),
            pltpu.VMEM((2,) + SLICES, F32),
            pltpu.VMEM((QUARTERS,) + SLICES, F32),
            pltpu.VMEM((ROWS, HID), F32),
            pltpu.VMEM((ROWS, HID), F32),
            pltpu.VMEM((ROWS, HID), F32),
            pltpu.VMEM((1,) + SLICES, BF16),
            pltpu.SemaphoreType.DMA((N_COPIES,)),
            pltpu.SemaphoreType.DMA((N_COPIES,)),
            pltpu.SemaphoreType.DMA((7,)),
        ],
        compiler_params=pltpu.CompilerParams(
            collective_id=0, has_side_effects=True, vmem_limit_bytes=int(51.85 * 2**20)
        ),
    )(*operands)


def finish(frag_ref, sums, anchor, momentum, master, one, two, up, master_o, one_o, two_o, up_o, anchor_o, momentum_o, buf, sem):
    pairs = ((master, master_o), (one, one_o), (two, two_o), (up, up_o))
    copies = [pltpu.make_async_copy(src, dst, sem.at[i]) for i, (src, dst) in enumerate(pairs)]
    for copy in copies:
        copy.start()
    frag = frag_ref[0]
    for quarter in range(QUARTERS):
        row = slice(quarter, quarter + 1)
        local_sum = sums[quarter, 0:1, :]
        anchor_f = anchor[0, row, :]
        momentum_f = momentum[0, row, :]
        for i in range(1, FRAGS):
            local_sum = jnp.where(frag == i, sums[quarter, i : i + 1, :], local_sum)
            anchor_f = jnp.where(frag == i, anchor[i, row, :], anchor_f)
            momentum_f = jnp.where(frag == i, momentum[i, row, :], momentum_f)
        buf[0, row, :], buf[1, row, :] = nesterov(anchor_f, momentum_f, anchor_f - local_sum * 0.25)
    for i, out in enumerate((anchor_o, momentum_o)):
        copies.append(pltpu.make_async_copy(buf.at[i], out, sem.at[4 + i]))
        copies[-1].start()
    for copy in copies:
        copy.wait()


def run_finish(*given):
    place = pl.BlockSpec(memory_space=pl.ANY)
    vmem = pl.BlockSpec(memory_space=pltpu.VMEM)
    small = jax.ShapeDtypeStruct((QUARTERS, 1024), F32)
    return pl.pallas_call(
        finish,
        name="finish",
        out_shape=RESULTS + (small, small),
        in_specs=[pl.BlockSpec(memory_space=pltpu.SMEM)] + [vmem] * 3 + [place] * 4,
        out_specs=(place,) * 6,
        scratch_shapes=[pltpu.VMEM((2, QUARTERS, 1024), F32), pltpu.SemaphoreType.DMA((6,))],
        compiler_params=pltpu.CompilerParams(vmem_limit_bytes=2**20),
    )(*given)


def local(
    tokens,
    cotangent,
    master,
    moment_one,
    moment_two,
    anchor,
    outer_momentum,
    local_frag,
    frag_index,
):
    *results, sums = run_exchange(tokens, cotangent, master, local_frag, moment_one, moment_two)
    return run_finish(frag_index, sums, anchor, outer_momentum, *results)


def solution(mesh):
    in_specs = (
        P("replica", "fsdp", None),
        P("replica", "fsdp", None),
        P("replica", "fsdp", None),
        P("replica", "fsdp", None),
        P("replica", "fsdp", None),
        P(None, None, "fsdp"),
        P(None, None, "fsdp"),
        P("replica", None, "fsdp"),
        P(),
    )
    out_specs = (
        P("replica", "fsdp", None),
        P("replica", "fsdp", None),
        P("replica", "fsdp", None),
        P("replica", "fsdp", None),
        P(None, "fsdp"),
        P(None, "fsdp"),
    )
    return jax.shard_map(local, mesh=mesh, in_specs=in_specs, out_specs=out_specs, check_vma=False)
```

```python
import jax
import jax.numpy as jnp
from jax import lax
from jax.experimental import pallas as pl
from jax.experimental.pallas import tpu as pltpu
from jax.sharding import PartitionSpec as P

MESH = pl.DeviceIdType.MESH
F32 = jnp.float32
BF16 = jnp.bfloat16

beta_one = 0.9
beta_two = 0.95
adam_eps = 1e-08
inner_rate = 0.0003
decay_rate = 0.1
correct_one = 1.0 - 0.9**20
correct_two = 1.0 - 0.95**20
outer_rate = 0.7
outer_mu = 0.9

NX = 4
NZ = 4
QUARTERS = 4
FRAGS = 4
TOK = 64
WIDE = 4096
COLS = WIDE // NX
HALF = COLS // 2
HID = 896
ROWS = 128
TBLK = QUARTERS * TOK
N_COPIES = 80


def adam_decayed(master, moment_one, moment_two):
    return (master * (1.0 - inner_rate * decay_rate), beta_one * moment_one, beta_two * moment_two)


def adam_update(master, moment_one, moment_two, grad):
    new_one = moment_one + (1.0 - beta_one) * grad
    new_two = moment_two + (1.0 - beta_two) * (grad * grad)
    scale = jnp.sqrt(new_two * (1.0 / correct_two)) + adam_eps
    new_master = master - (inner_rate / correct_one) * (new_one / scale)
    return (new_master, new_one, new_two)


def nesterov(anchor_part, momentum_part, delta):
    new_momentum = outer_mu * momentum_part + delta
    new_anchor = anchor_part - outer_rate * (outer_mu * new_momentum + delta)
    return (new_anchor, new_momentum)


def mult(value, by):
    return pl.multiple_of(value, by)


ORDER_ONE = ("t0_own t0_xp t0_xm t0_x2 w_own w_pa w_mb w_c0 t1_own c_pa c_mb t0_on3 t0_on1 t0_on2 o1 t1_xp t1_xm t1_x2 t0_re0 c_pb c_ma t0_re3 t0_re1 t0_re2 t1_on3 t1_on1 t1_on2 o2 w_ra w_rb t1_re0 c_ra c_rb t1_re3 w_pb w_ma t1_re1 t1_re2 o3",)
ORDER_TWO = ("w_c3 w_c1",)
ORDER_THREE = ("w_c2a w_c2b",)


class Sent:
    def __init__(self, copy):
        self.copy = copy
        self.here = False

    def wait_recv(self):
        if not self.here:
            self.here = True
            self.copy.wait_recv()


def exchange(
    tok,
    cot,
    master,
    local_hbm,
    one_hbm,
    two_hbm,
    master_out,
    one_out,
    two_out,
    up_out,
    sum_out,
    tbuf,
    wbuf,
    cbuf,
    acc,
    upf,
    up_far,
    up_near,
    up_in,
    up_got,
    g_core,
    g_core_in,
    g_far,
    g_near,
    g_in,
    g_got,
    o_part,
    o_in,
    o_all,
    master_v,
    one_v,
    two_v,
    local_frag,
    ssem,
    rsem,
    lsem,
):
    fs = lax.axis_index("fsdp")
    rp = lax.axis_index("replica")
    x, zh, k = fs // 8, lax.rem(fs // 2, 4), lax.rem(fs, 2)
    y, zl = rp // 2, lax.rem(rp, 2)
    yl = lax.rem(y, 2)
    c = lax.rem(rp, 4)
    c_l = 2 * yl + (1 - zl)

    def at(dx=0, dz=0, core=k, yy=y, ll=zl):
        return (lax.rem(x + dx, 4) * 8 + lax.rem(zh + dz, 4) * 2 + core, yy * 2 + ll)

    def flip(bit):
        return y + bit * (1 - 2 * lax.rem(y // bit, 2))

    xp, x2, xm = at(1), at(2), at(3)
    zp, zm = at(0, 1), at(0, 3)
    co = at(core=1 - k)
    py, pl_ = at(yy=flip(1)), at(ll=1 - zl)
    y2, y4 = at(yy=flip(2)), at(yy=flip(4))

    barrier = pltpu.get_barrier_semaphore()
    partners = (xp, x2, xm, zp, zm, co, py, pl_, y2, y4)
    for partner in partners:
        pl.semaphore_signal(barrier, inc=1, device_id=partner, device_id_type=MESH)

    started = []

    def send(src, dst, to):
        number = len(started)
        copy = pltpu.make_async_remote_copy(
            src_ref=src,
            dst_ref=dst,
            send_sem=ssem.at[number],
            recv_sem=rsem.at[number],
            device_id=to,
            device_id_type=MESH,
        )
        copy.start()
        started.append(Sent(copy))
        return started[-1]

    own_pair = zh // 2
    pairs = (1 - own_pair, own_pair)

    def trow(rnd, slot, quarter):
        return tbuf.at[rnd, pl.ds(mult(slot * TBLK + quarter * TOK, TOK), TOK), :]

    def piece(rnd, dx):
        return tok.at[0, :, pl.ds(mult(lax.rem(x + dx, 4) * COLS + pairs[rnd] * HALF, HALF), HALF)]

    def woff(dz, core):
        return lax.rem(zh + dz, 4) * (2 * ROWS) + core * ROWS

    def whalf(dz, half):
        return wbuf.at[pl.ds(mult(woff(dz, k) + half * (ROWS // 2), ROWS // 2), ROWS // 2), :]

    def wfull(dz):
        return wbuf.at[pl.ds(mult(woff(dz, k), ROWS), ROWS), :]

    def chalf(slot, half):
        return cbuf.at[pl.ds(slot * TBLK + half * (TBLK // 2), TBLK // 2), :]

    def own_chalf(half):
        return cot.at[0, pl.ds(half * (TBLK // 2), TBLK // 2), :]

    loads = [
        pltpu.make_async_copy(src, dst, lsem.at[i])
        for i, (src, dst) in enumerate(
            (
                (master.at[0], master_v),
                (piece(0, 0), trow(0, 0, c)),
                (piece(1, 0), trow(1, 0, c)),
                (local_hbm, local_frag),
                (cot.at[0], cbuf.at[pl.ds(0, TBLK), :]),
                (one_hbm.at[0], one_v),
                (two_hbm.at[0], two_v),
            )
        )
    ]
    for load in loads:
        load.start()
    l_master, l_tok, l_tok2, l_local, l_cot, l_one, l_two = loads

    pl.semaphore_wait(barrier, len(partners))

    t_y, t_l, t_r = {}, {}, {}

    cp = {}

    def own_outer():
        for load in (l_tok, l_tok2, l_local, l_cot, l_one, l_two):
            load.wait()
        o_part[0] = local_frag[0].astype(F32)
        cp["o1"] = send(o_part.at[0], o_in.at[0], y2)

    def outer_two():
        cp["o1"].wait_recv()
        o_part[1] = o_part[0] + o_in[0]
        cp["o2"] = send(o_part.at[1], o_in.at[1], y4)

    def outer_three():
        cp["o2"].wait_recv()
        o_all[c] = o_part[1] + o_in[1]
        cp["o3"] = send(o_all.at[c], o_all.at[c], pl_)

    def outer_four():
        cp["o3"].wait_recv()
        o_two = pl.ds(2 * yl, 2)
        cp["o4"] = send(o_all.at[o_two], o_all.at[o_two], py)

    def put(name, src, dst, to):
        def step():
            cp[name] = send(src, dst, to)

        return step

    def after(name, *steps):
        def step():
            cp[name].wait_recv()
            for each in steps:
                each()

        return step

    def t_on(rnd, slot):
        def step():
            t_l[rnd, slot] = send(trow(rnd, slot, c), trow(rnd, slot, c), pl_)
            t_y[rnd, slot] = send(trow(rnd, slot, c), trow(rnd, slot, c), py)

        return step

    def t_relay(rnd, slot):
        def step():
            t_l[rnd, slot].wait_recv()
            t_r[rnd, slot] = send(trow(rnd, slot, c_l), trow(rnd, slot, c_l), py)

        return step

    def t_own(rnd):
        def step():
            t_y[rnd, 0] = send(piece(rnd, 0), trow(rnd, 0, c), py)
            t_l[rnd, 0] = send(piece(rnd, 0), trow(rnd, 0, c), pl_)

        return step

    def own_rows():
        l_master.wait()
        wbuf[pl.ds(mult(woff(0, k), ROWS), ROWS), :] = master_v[...].astype(BF16)

    steps = {
        "w_own": own_rows,
        "w_pa": put("w_pa", whalf(0, 0), whalf(0, 0), zp),
        "w_mb": put("w_mb", whalf(0, 1), whalf(0, 1), zm),
        "w_pb": put("w_pb", whalf(0, 1), whalf(0, 1), zp),
        "w_ma": put("w_ma", whalf(0, 0), whalf(0, 0), zm),
        "w_ra": after("w_pa", put("w_ra", whalf(3, 0), whalf(3, 0), zp)),
        "w_rb": after("w_mb", put("w_rb", whalf(1, 1), whalf(1, 1), zm)),
        "w_c0": put("w_c0", wfull(0), wfull(0), co),
        "w_c3": after("w_pb", put("w_c3", wfull(3), wfull(3), co)),
        "w_c1": after("w_ma", put("w_c1", wfull(1), wfull(1), co)),
        "w_c2a": after("w_ra", put("w_c2a", whalf(2, 0), whalf(2, 0), co)),
        "w_c2b": after("w_rb", put("w_c2b", whalf(2, 1), whalf(2, 1), co)),
        "c_pa": put("c_pa", own_chalf(0), chalf(3, 0), xp),
        "c_mb": put("c_mb", own_chalf(1), chalf(1, 1), xm),
        "c_pb": put("c_pb", own_chalf(1), chalf(3, 1), xp),
        "c_ma": put("c_ma", own_chalf(0), chalf(1, 0), xm),
        "c_ra": after("c_pa", put("c_ra", chalf(3, 0), chalf(2, 0), xp)),
        "c_rb": after("c_mb", put("c_rb", chalf(1, 1), chalf(2, 1), xm)),
        "o1": own_outer,
        "o2": outer_two,
        "o3": outer_three,
        "o4": outer_four,
    }
    for r in range(2):
        steps[f"t{r}_own"] = t_own(r)
        for slot, name, to in ((3, "xp", xp), (1, "xm", xm), (2, "x2", x2)):
            steps[f"t{r}_{name}"] = put(f"t{r}_{name}", piece(r, 4 - slot), trow(r, slot, c), to)
            steps[f"t{r}_on{slot}"] = after(f"t{r}_{name}", t_on(r, slot))
        for slot in range(NX):
            steps[f"t{r}_re{slot}"] = t_relay(r, slot)

    def run(order):
        for step in " ".join(order).split():
            steps[step]()

    run(ORDER_ONE)

    half_t = TBLK // 2
    half_r = ROWS // 2
    odd = lax.rem(zh, 2)
    far = lax.rem(zh + 2, 4)
    blocks = (far, 3 - zh, zh + 1 - 2 * odd, zh)
    core_copies = []

    def tokens_here(rnd, slot):
        t_y[rnd, slot].wait_recv()
        t_r[rnd, slot].wait_recv()

    def grad_part(i, lo, hi):
        rnd = i // 2
        col = pl.ds(mult(lax.rem(blocks[i], 2) * 256, 256), 256)
        left = tbuf[rnd, lo * TBLK : hi * TBLK, col]
        right = cbuf[lo * TBLK : hi * TBLK, :]
        return lax.dot_general(left, right, (((0,), (0,)), ((), ())), preferred_element_type=F32)

    def both_rows(i):
        return pl.ds(mult(blocks[i] * 2 * ROWS, 2 * ROWS), 2 * ROWS)

    def rows_of(i, core):
        return pl.ds(mult(blocks[i] * 2 * ROWS + core * ROWS, ROWS), ROWS)

    def core_send(i):
        g_core[i] = acc[rows_of(i, 1 - k), :].astype(BF16)
        core_copies.append(send(g_core.at[i], g_core_in.at[i], co))

    def core_sum(i):
        core_copies[i].wait_recv()
        total = acc[rows_of(i, k), :] + g_core_in[i].astype(F32)
        acc[rows_of(i, k), :] = total
        return total

    def up_part(slot, store):
        rows = slice(slot * TBLK, (slot + 1) * TBLK)
        for lo in range(0, HID, 256):
            hi = min(lo + 256, HID)
            total = None
            for rnd in range(2):
                weights = wbuf[pl.ds(mult(pairs[rnd] * HALF, HALF), HALF), lo:hi]
                part = jnp.dot(tbuf[rnd, rows, :], weights, preferred_element_type=F32)
                total = part if total is None else total + part
            store(lo, hi, total)

    for name in ("c_ra", "c_rb", "c_pb", "c_ma"):
        cp[name].wait_recv()
    for slot in range(NX):
        tokens_here(0, slot)
    for i in (0, 1):
        acc[both_rows(i), :] = grad_part(i, 0, NX)
        core_send(i)
    run(ORDER_TWO)
    g_far[...] = core_sum(0).astype(BF16)
    g_fp = send(g_far.at[pl.ds(0, half_r), :], g_in.at[0], zp)
    g_fm = send(g_far.at[pl.ds(half_r, half_r), :], g_in.at[1], zm)
    core_sum(1)
    run(ORDER_THREE)

    def store_far(lo, hi, value):
        up_far[:, lo:hi] = value.astype(BF16)

    def store_f(i):
        def store(lo, hi, value):
            upf[i, :, lo:hi] = value

        return store

    master_v[...], one_v[...], two_v[...] = adam_decayed(master_v[...], one_v[...], two_v[...])
    for name in ("w_c0", "w_c1", "w_c3", "w_c2a", "w_c2b"):
        cp[name].wait_recv()
    tokens_here(1, 2)
    up_part(2, store_far)
    u_fp = send(up_far.at[pl.ds(0, half_t), :], up_in.at[0], xp)
    u_fm = send(up_far.at[pl.ds(half_t, half_t), :], up_in.at[1], xm)

    tokens_here(1, 0)
    tokens_here(1, 1)
    tokens_here(1, 3)
    for i in (2, 3):
        acc[both_rows(i), :] = grad_part(i, 0, NX)
        core_send(i)

    up_part(3, store_f(2))
    up_near[1, :half_t, :] = upf[2, :half_t, :].astype(BF16)
    u_ma = send(up_near.at[1, pl.ds(0, half_t), :], up_got.at[1, pl.ds(0, half_t), :], xm)

    core_sum(2)
    near = [pl.ds(mult(woff(e, k), ROWS), ROWS) for e in (1, 3)]
    g_near[0] = acc[near[0], :].astype(BF16)
    g_pb = send(g_near.at[0, pl.ds(half_r, half_r), :], g_got.at[0, pl.ds(half_r, half_r), :], zp)
    g_near[1] = acc[near[1], :].astype(BF16)
    g_ma = send(g_near.at[1, pl.ds(0, half_r), :], g_got.at[1, pl.ds(0, half_r), :], zm)

    steps["o4"]()
    up_part(1, store_f(1))
    up_near[0, half_t:, :] = upf[1, half_t:, :].astype(BF16)
    u_pb = send(up_near.at[0, pl.ds(half_t, half_t), :], up_got.at[0, pl.ds(half_t, half_t), :], xp)
    def row_half(dz, half):
        return pl.ds(mult(woff(dz, k) + half * half_r, half_r), half_r)

    g_fp.wait_recv()
    g_near[0, :half_r, :] = (acc[row_half(1, 0), :] + g_in[0].astype(F32)).astype(BF16)
    g_pa = send(g_near.at[0, pl.ds(0, half_r), :], g_got.at[0, pl.ds(0, half_r), :], zp)
    g_fm.wait_recv()
    g_near[1, half_r:, :] = (acc[row_half(3, 1), :] + g_in[1].astype(F32)).astype(BF16)
    g_mb = send(g_near.at[1, pl.ds(half_r, half_r), :], g_got.at[1, pl.ds(half_r, half_r), :], zm)

    u_fm.wait_recv()
    up_near[1, half_t:, :] = (upf[2, half_t:, :] + up_in[1].astype(F32)).astype(BF16)
    u_mb = send(up_near.at[1, pl.ds(half_t, half_t), :], up_got.at[1, pl.ds(half_t, half_t), :], xm)
    u_fp.wait_recv()
    up_near[0, :half_t, :] = (upf[1, :half_t, :] + up_in[0].astype(F32)).astype(BF16)
    u_pa = send(up_near.at[0, pl.ds(0, half_t), :], up_got.at[0, pl.ds(0, half_t), :], xp)
    up_part(0, store_f(0))
    core_sum(3)
    cp["o4"].wait_recv()
    sum_out[...] = o_all[...]

    for copy in (g_pb, g_ma, g_pa, g_mb):
        copy.wait_recv()
    own = pl.ds(mult(woff(0, k), ROWS), ROWS)
    grad = acc[own, :] + g_got[0].astype(F32) + g_got[1].astype(F32)
    master_out[0], one_out[0], two_out[0] = adam_update(master_v[...], one_v[...], two_v[...], grad)

    for copy in (u_pb, u_ma, u_pa, u_mb):
        copy.wait_recv()
    up_out[0] = (upf[0] + up_got[0].astype(F32) + up_got[1].astype(F32)).astype(BF16)

    for sent in started:
        sent.copy.wait_send()


STATE = jax.ShapeDtypeStruct((1, ROWS, HID), F32)
RESULTS = (
    STATE,
    STATE,
    STATE,
    jax.ShapeDtypeStruct((1, TBLK, HID), BF16),
)
SLICES = (FRAGS, 1024)


def run_exchange(*operands):
    vmem = pl.BlockSpec(memory_space=pltpu.VMEM)
    return pl.pallas_call(
        exchange,
        name="exchange",
        out_shape=RESULTS + (jax.ShapeDtypeStruct((QUARTERS,) + SLICES, F32),),
        in_specs=[pl.BlockSpec(memory_space=pl.ANY)] * 6,
        out_specs=(vmem,) * 5,
        scratch_shapes=[
            pltpu.VMEM((2, NX * TBLK, HALF), BF16),
            pltpu.VMEM((COLS, HID), BF16),
            pltpu.VMEM((NX * TBLK, HID), BF16),
            pltpu.VMEM((COLS, HID), F32),
            pltpu.VMEM((3, TBLK, HID), F32),
            pltpu.VMEM((TBLK, HID), BF16),
            pltpu.VMEM((2, TBLK, HID), BF16),
            pltpu.VMEM((2, TBLK // 2, HID), BF16),
            pltpu.VMEM((2, TBLK, HID), BF16),
            pltpu.VMEM((4, ROWS, HID), BF16),
            pltpu.VMEM((4, ROWS, HID), BF16),
            pltpu.VMEM((ROWS, HID), BF16),
            pltpu.VMEM((2, ROWS, HID), BF16),
            pltpu.VMEM((2, ROWS // 2, HID), BF16),
            pltpu.VMEM((2, ROWS, HID), BF16),
            pltpu.VMEM((2,) + SLICES, F32),
            pltpu.VMEM((2,) + SLICES, F32),
            pltpu.VMEM((QUARTERS,) + SLICES, F32),
            pltpu.VMEM((ROWS, HID), F32),
            pltpu.VMEM((ROWS, HID), F32),
            pltpu.VMEM((ROWS, HID), F32),
            pltpu.VMEM((1,) + SLICES, BF16),
            pltpu.SemaphoreType.DMA((N_COPIES,)),
            pltpu.SemaphoreType.DMA((N_COPIES,)),
            pltpu.SemaphoreType.DMA((7,)),
        ],
        compiler_params=pltpu.CompilerParams(
            collective_id=0, has_side_effects=True, vmem_limit_bytes=int(51.85 * 2**20)
        ),
    )(*operands)


def finish(frag_ref, sums, anchor, momentum, master, one, two, up, master_o, one_o, two_o, up_o, anchor_o, momentum_o, buf, sem):
    pairs = ((master, master_o), (one, one_o), (two, two_o), (up, up_o))
    copies = [pltpu.make_async_copy(src, dst, sem.at[i]) for i, (src, dst) in enumerate(pairs)]
    for copy in copies:
        copy.start()
    frag = frag_ref[0]
    for quarter in range(QUARTERS):
        row = slice(quarter, quarter + 1)
        local_sum = sums[quarter, 0:1, :]
        anchor_f = anchor[0, row, :]
        momentum_f = momentum[0, row, :]
        for i in range(1, FRAGS):
            local_sum = jnp.where(frag == i, sums[quarter, i : i + 1, :], local_sum)
            anchor_f = jnp.where(frag == i, anchor[i, row, :], anchor_f)
            momentum_f = jnp.where(frag == i, momentum[i, row, :], momentum_f)
        buf[0, row, :], buf[1, row, :] = nesterov(anchor_f, momentum_f, anchor_f - local_sum * 0.25)
    for i, out in enumerate((anchor_o, momentum_o)):
        copies.append(pltpu.make_async_copy(buf.at[i], out, sem.at[4 + i]))
        copies[-1].start()
    for copy in copies:
        copy.wait()


def run_finish(*given):
    place = pl.BlockSpec(memory_space=pl.ANY)
    vmem = pl.BlockSpec(memory_space=pltpu.VMEM)
    small = jax.ShapeDtypeStruct((QUARTERS, 1024), F32)
    return pl.pallas_call(
        finish,
        name="finish",
        out_shape=RESULTS + (small, small),
        in_specs=[pl.BlockSpec(memory_space=pltpu.SMEM)] + [vmem] * 3 + [place] * 4,
        out_specs=(place,) * 6,
        scratch_shapes=[pltpu.VMEM((2, QUARTERS, 1024), F32), pltpu.SemaphoreType.DMA((6,))],
        compiler_params=pltpu.CompilerParams(vmem_limit_bytes=2**20),
    )(*given)


def local(
    tokens,
    cotangent,
    master,
    moment_one,
    moment_two,
    anchor,
    outer_momentum,
    local_frag,
    frag_index,
):
    *results, sums = run_exchange(tokens, cotangent, master, local_frag, moment_one, moment_two)
    return run_finish(frag_index, sums, anchor, outer_momentum, *results)


def solution(mesh):
    in_specs = (
        P("replica", "fsdp", None),
        P("replica", "fsdp", None),
        P("replica", "fsdp", None),
        P("replica", "fsdp", None),
        P("replica", "fsdp", None),
        P(None, None, "fsdp"),
        P(None, None, "fsdp"),
        P("replica", None, "fsdp"),
        P(),
    )
    out_specs = (
        P("replica", "fsdp", None),
        P("replica", "fsdp", None),
        P("replica", "fsdp", None),
        P("replica", "fsdp", None),
        P(None, "fsdp"),
        P(None, "fsdp"),
    )
    return jax.shard_map(local, mesh=mesh, in_specs=in_specs, out_specs=out_specs, check_vma=False)
```

```python
import jax
import jax.numpy as jnp
from jax import lax
from jax.experimental import pallas as pl
from jax.experimental.pallas import tpu as pltpu
from jax.sharding import PartitionSpec as P

MESH = pl.DeviceIdType.MESH
F32 = jnp.float32
BF16 = jnp.bfloat16

beta_one = 0.9
beta_two = 0.95
adam_eps = 1e-08
inner_rate = 0.0003
decay_rate = 0.1
correct_one = 1.0 - 0.9**20
correct_two = 1.0 - 0.95**20
outer_rate = 0.7
outer_mu = 0.9

NX = 4
NZ = 4
QUARTERS = 4
FRAGS = 4
TOK = 64
WIDE = 4096
COLS = WIDE // NX
HALF = COLS // 2
HID = 896
ROWS = 128
TBLK = QUARTERS * TOK
N_COPIES = 80


def adam_decayed(master, moment_one, moment_two):
    return (master * (1.0 - inner_rate * decay_rate), beta_one * moment_one, beta_two * moment_two)


def adam_update(master, moment_one, moment_two, grad):
    new_one = moment_one + (1.0 - beta_one) * grad
    new_two = moment_two + (1.0 - beta_two) * (grad * grad)
    scale = jnp.sqrt(new_two * (1.0 / correct_two)) + adam_eps
    new_master = master - (inner_rate / correct_one) * (new_one / scale)
    return (new_master, new_one, new_two)


def nesterov(anchor_part, momentum_part, delta):
    new_momentum = outer_mu * momentum_part + delta
    new_anchor = anchor_part - outer_rate * (outer_mu * new_momentum + delta)
    return (new_anchor, new_momentum)


def mult(value, by):
    return pl.multiple_of(value, by)


ORDER_ONE = (
    "t0_own", "t0_xp", "t0_xm", "t0_x2", "w_own", "w_pa", "w_mb", "w_c0", "t1_own", "c_pa", "c_mb", "t0_on3",
    "t0_on1", "t0_on2", "o1", "t1_xp", "t1_xm", "t1_x2", "t0_re0", "c_pb", "c_ma", "t0_re3", "t0_re1", "t0_re2",
    "t1_on3", "t1_on1", "t1_on2", "o2", "w_ra", "w_rb", "t1_re0", "c_ra", "c_rb", "t1_re3", "w_pb", "w_ma", "t1_re1",
    "t1_re2", "o3",
)
ORDER_TWO = ("w_c3", "w_c1")
ORDER_THREE = ("w_c2a", "w_c2b")


class Sent:
    def __init__(self, copy):
        self.copy = copy
        self.here = False

    def wait_recv(self):
        if not self.here:
            self.here = True
            self.copy.wait_recv()


def exchange(
    tok,
    cot,
    master,
    local_hbm,
    one_hbm,
    two_hbm,
    master_out,
    one_out,
    two_out,
    up_out,
    sum_out,
    tbuf,
    wbuf,
    cbuf,
    acc,
    upf,
    up_far,
    up_near,
    up_in,
    up_got,
    g_core,
    g_core_in,
    g_far,
    g_near,
    g_in,
    g_got,
    o_part,
    o_in,
    o_all,
    master_v,
    one_v,
    two_v,
    local_frag,
    ssem,
    rsem,
    lsem,
):
    fs = lax.axis_index("fsdp")
    rp = lax.axis_index("replica")
    x, zh, k = fs // 8, lax.rem(fs // 2, 4), lax.rem(fs, 2)
    y, zl = rp // 2, lax.rem(rp, 2)
    yl = lax.rem(y, 2)
    c = lax.rem(rp, 4)
    c_l = 2 * yl + (1 - zl)

    def at(dx=0, dz=0, core=k, yy=y, ll=zl):
        return (lax.rem(x + dx, 4) * 8 + lax.rem(zh + dz, 4) * 2 + core, yy * 2 + ll)

    def flip(bit):
        return y + bit * (1 - 2 * lax.rem(y // bit, 2))

    xp, x2, xm = at(1), at(2), at(3)
    zp, zm = at(0, 1), at(0, 3)
    co = at(core=1 - k)
    py, pl_ = at(yy=flip(1)), at(ll=1 - zl)
    y2, y4 = at(yy=flip(2)), at(yy=flip(4))

    barrier = pltpu.get_barrier_semaphore()
    partners = (xp, x2, xm, zp, zm, co, py, pl_, y2, y4)
    for partner in partners:
        pl.semaphore_signal(barrier, inc=1, device_id=partner, device_id_type=MESH)

    started = []

    def send(src, dst, to):
        number = len(started)
        copy = pltpu.make_async_remote_copy(
            src_ref=src,
            dst_ref=dst,
            send_sem=ssem.at[number],
            recv_sem=rsem.at[number],
            device_id=to,
            device_id_type=MESH,
        )
        copy.start()
        started.append(Sent(copy))
        return started[-1]

    own_pair = zh // 2
    pairs = (1 - own_pair, own_pair)

    def trow(rnd, slot, quarter):
        return tbuf.at[rnd, pl.ds(mult(slot * TBLK + quarter * TOK, TOK), TOK), :]

    def piece(rnd, dx):
        return tok.at[0, :, pl.ds(mult(lax.rem(x + dx, 4) * COLS + pairs[rnd] * HALF, HALF), HALF)]

    def woff(dz, core):
        return lax.rem(zh + dz, 4) * (2 * ROWS) + core * ROWS

    def whalf(dz, half):
        return wbuf.at[pl.ds(mult(woff(dz, k) + half * (ROWS // 2), ROWS // 2), ROWS // 2), :]

    def wfull(dz):
        return wbuf.at[pl.ds(mult(woff(dz, k), ROWS), ROWS), :]

    def chalf(slot, half):
        return cbuf.at[pl.ds(slot * TBLK + half * (TBLK // 2), TBLK // 2), :]

    def own_chalf(half):
        return cot.at[0, pl.ds(half * (TBLK // 2), TBLK // 2), :]

    loads = [
        pltpu.make_async_copy(src, dst, lsem.at[i])
        for i, (src, dst) in enumerate(
            (
                (master.at[0], master_v),
                (piece(0, 0), trow(0, 0, c)),
                (piece(1, 0), trow(1, 0, c)),
                (local_hbm, local_frag),
                (cot.at[0], cbuf.at[pl.ds(0, TBLK), :]),
                (one_hbm.at[0], one_v),
                (two_hbm.at[0], two_v),
            )
        )
    ]
    for load in loads:
        load.start()
    l_master, l_tok, l_tok2, l_local, l_cot, l_one, l_two = loads

    pl.semaphore_wait(barrier, len(partners))

    t_y, t_l, t_r = {}, {}, {}

    cp = {}

    def own_outer():
        for load in (l_tok, l_tok2, l_local, l_cot, l_one, l_two):
            load.wait()
        o_part[0] = local_frag[0].astype(F32)
        cp["o1"] = send(o_part.at[0], o_in.at[0], y2)

    def outer_two():
        cp["o1"].wait_recv()
        o_part[1] = o_part[0] + o_in[0]
        cp["o2"] = send(o_part.at[1], o_in.at[1], y4)

    def outer_three():
        cp["o2"].wait_recv()
        o_all[c] = o_part[1] + o_in[1]
        cp["o3"] = send(o_all.at[c], o_all.at[c], pl_)

    def outer_four():
        cp["o3"].wait_recv()
        o_two = pl.ds(2 * yl, 2)
        cp["o4"] = send(o_all.at[o_two], o_all.at[o_two], py)

    def put(name, src, dst, to):
        def step():
            cp[name] = send(src, dst, to)

        return step

    def after(name, *steps):
        def step():
            cp[name].wait_recv()
            for each in steps:
                each()

        return step

    def t_on(rnd, slot):
        def step():
            t_l[rnd, slot] = send(trow(rnd, slot, c), trow(rnd, slot, c), pl_)
            t_y[rnd, slot] = send(trow(rnd, slot, c), trow(rnd, slot, c), py)

        return step

    def t_relay(rnd, slot):
        def step():
            t_l[rnd, slot].wait_recv()
            t_r[rnd, slot] = send(trow(rnd, slot, c_l), trow(rnd, slot, c_l), py)

        return step

    def t_own(rnd):
        def step():
            t_y[rnd, 0] = send(piece(rnd, 0), trow(rnd, 0, c), py)
            t_l[rnd, 0] = send(piece(rnd, 0), trow(rnd, 0, c), pl_)

        return step

    def own_rows():
        l_master.wait()
        wbuf[pl.ds(mult(woff(0, k), ROWS), ROWS), :] = master_v[...].astype(BF16)

    steps = {
        "w_own": own_rows,
        "w_pa": put("w_pa", whalf(0, 0), whalf(0, 0), zp),
        "w_mb": put("w_mb", whalf(0, 1), whalf(0, 1), zm),
        "w_pb": put("w_pb", whalf(0, 1), whalf(0, 1), zp),
        "w_ma": put("w_ma", whalf(0, 0), whalf(0, 0), zm),
        "w_ra": after("w_pa", put("w_ra", whalf(3, 0), whalf(3, 0), zp)),
        "w_rb": after("w_mb", put("w_rb", whalf(1, 1), whalf(1, 1), zm)),
        "w_c0": put("w_c0", wfull(0), wfull(0), co),
        "w_c3": after("w_pb", put("w_c3", wfull(3), wfull(3), co)),
        "w_c1": after("w_ma", put("w_c1", wfull(1), wfull(1), co)),
        "w_c2a": after("w_ra", put("w_c2a", whalf(2, 0), whalf(2, 0), co)),
        "w_c2b": after("w_rb", put("w_c2b", whalf(2, 1), whalf(2, 1), co)),
        "c_pa": put("c_pa", own_chalf(0), chalf(3, 0), xp),
        "c_mb": put("c_mb", own_chalf(1), chalf(1, 1), xm),
        "c_pb": put("c_pb", own_chalf(1), chalf(3, 1), xp),
        "c_ma": put("c_ma", own_chalf(0), chalf(1, 0), xm),
        "c_ra": after("c_pa", put("c_ra", chalf(3, 0), chalf(2, 0), xp)),
        "c_rb": after("c_mb", put("c_rb", chalf(1, 1), chalf(2, 1), xm)),
        "o1": own_outer,
        "o2": outer_two,
        "o3": outer_three,
        "o4": outer_four,
    }
    for r in range(2):
        steps[f"t{r}_own"] = t_own(r)
        for slot, name, to in ((3, "xp", xp), (1, "xm", xm), (2, "x2", x2)):
            steps[f"t{r}_{name}"] = put(f"t{r}_{name}", piece(r, 4 - slot), trow(r, slot, c), to)
            steps[f"t{r}_on{slot}"] = after(f"t{r}_{name}", t_on(r, slot))
        for slot in range(NX):
            steps[f"t{r}_re{slot}"] = t_relay(r, slot)

    def run(order):
        for step in order:
            steps[step]()

    run(ORDER_ONE)

    half_t = TBLK // 2
    half_r = ROWS // 2
    odd = lax.rem(zh, 2)
    far = lax.rem(zh + 2, 4)
    blocks = (far, 3 - zh, zh + 1 - 2 * odd, zh)
    core_copies = []

    def tokens_here(rnd, slot):
        t_y[rnd, slot].wait_recv()
        t_r[rnd, slot].wait_recv()

    def grad_part(i, lo, hi):
        rnd = i // 2
        col = pl.ds(mult(lax.rem(blocks[i], 2) * 256, 256), 256)
        left = tbuf[rnd, lo * TBLK : hi * TBLK, col]
        right = cbuf[lo * TBLK : hi * TBLK, :]
        return lax.dot_general(left, right, (((0,), (0,)), ((), ())), preferred_element_type=F32)

    def both_rows(i):
        return pl.ds(mult(blocks[i] * 2 * ROWS, 2 * ROWS), 2 * ROWS)

    def rows_of(i, core):
        return pl.ds(mult(blocks[i] * 2 * ROWS + core * ROWS, ROWS), ROWS)

    def core_send(i):
        g_core[i] = acc[rows_of(i, 1 - k), :].astype(BF16)
        core_copies.append(send(g_core.at[i], g_core_in.at[i], co))

    def core_sum(i):
        core_copies[i].wait_recv()
        total = acc[rows_of(i, k), :] + g_core_in[i].astype(F32)
        acc[rows_of(i, k), :] = total
        return total

    def up_part(slot, store):
        rows = slice(slot * TBLK, (slot + 1) * TBLK)
        for lo in range(0, HID, 256):
            hi = min(lo + 256, HID)
            total = None
            for rnd in range(2):
                weights = wbuf[pl.ds(mult(pairs[rnd] * HALF, HALF), HALF), lo:hi]
                part = jnp.dot(tbuf[rnd, rows, :], weights, preferred_element_type=F32)
                total = part if total is None else total + part
            store(lo, hi, total)

    for name in ("c_ra", "c_rb", "c_pb", "c_ma"):
        cp[name].wait_recv()
    for slot in range(NX):
        tokens_here(0, slot)
    for i in (0, 1):
        acc[both_rows(i), :] = grad_part(i, 0, NX)
        core_send(i)
    run(ORDER_TWO)
    g_far[...] = core_sum(0).astype(BF16)
    g_fp = send(g_far.at[pl.ds(0, half_r), :], g_in.at[0], zp)
    g_fm = send(g_far.at[pl.ds(half_r, half_r), :], g_in.at[1], zm)
    core_sum(1)
    run(ORDER_THREE)

    def store_far(lo, hi, value):
        up_far[:, lo:hi] = value.astype(BF16)

    def store_f(i):
        def store(lo, hi, value):
            upf[i, :, lo:hi] = value

        return store

    master_v[...], one_v[...], two_v[...] = adam_decayed(master_v[...], one_v[...], two_v[...])
    for name in ("w_c0", "w_c1", "w_c3", "w_c2a", "w_c2b"):
        cp[name].wait_recv()
    tokens_here(1, 2)
    up_part(2, store_far)
    u_fp = send(up_far.at[pl.ds(0, half_t), :], up_in.at[0], xp)
    u_fm = send(up_far.at[pl.ds(half_t, half_t), :], up_in.at[1], xm)

    tokens_here(1, 0)
    tokens_here(1, 1)
    tokens_here(1, 3)
    for i in (2, 3):
        acc[both_rows(i), :] = grad_part(i, 0, NX)
        core_send(i)

    up_part(3, store_f(2))
    up_near[1, :half_t, :] = upf[2, :half_t, :].astype(BF16)
    u_ma = send(up_near.at[1, pl.ds(0, half_t), :], up_got.at[1, pl.ds(0, half_t), :], xm)

    core_sum(2)
    near = [pl.ds(mult(woff(e, k), ROWS), ROWS) for e in (1, 3)]
    g_near[0] = acc[near[0], :].astype(BF16)
    g_pb = send(g_near.at[0, pl.ds(half_r, half_r), :], g_got.at[0, pl.ds(half_r, half_r), :], zp)
    g_near[1] = acc[near[1], :].astype(BF16)
    g_ma = send(g_near.at[1, pl.ds(0, half_r), :], g_got.at[1, pl.ds(0, half_r), :], zm)

    steps["o4"]()
    up_part(1, store_f(1))
    up_near[0, half_t:, :] = upf[1, half_t:, :].astype(BF16)
    u_pb = send(up_near.at[0, pl.ds(half_t, half_t), :], up_got.at[0, pl.ds(half_t, half_t), :], xp)
    def row_half(dz, half):
        return pl.ds(mult(woff(dz, k) + half * half_r, half_r), half_r)

    g_fp.wait_recv()
    g_near[0, :half_r, :] = (acc[row_half(1, 0), :] + g_in[0].astype(F32)).astype(BF16)
    g_pa = send(g_near.at[0, pl.ds(0, half_r), :], g_got.at[0, pl.ds(0, half_r), :], zp)
    g_fm.wait_recv()
    g_near[1, half_r:, :] = (acc[row_half(3, 1), :] + g_in[1].astype(F32)).astype(BF16)
    g_mb = send(g_near.at[1, pl.ds(half_r, half_r), :], g_got.at[1, pl.ds(half_r, half_r), :], zm)

    u_fm.wait_recv()
    up_near[1, half_t:, :] = (upf[2, half_t:, :] + up_in[1].astype(F32)).astype(BF16)
    u_mb = send(up_near.at[1, pl.ds(half_t, half_t), :], up_got.at[1, pl.ds(half_t, half_t), :], xm)
    u_fp.wait_recv()
    up_near[0, :half_t, :] = (upf[1, :half_t, :] + up_in[0].astype(F32)).astype(BF16)
    u_pa = send(up_near.at[0, pl.ds(0, half_t), :], up_got.at[0, pl.ds(0, half_t), :], xp)
    up_part(0, store_f(0))
    core_sum(3)
    cp["o4"].wait_recv()
    sum_out[...] = o_all[...]

    for copy in (g_pb, g_ma, g_pa, g_mb):
        copy.wait_recv()
    own = pl.ds(mult(woff(0, k), ROWS), ROWS)
    grad = acc[own, :] + g_got[0].astype(F32) + g_got[1].astype(F32)
    master_out[0], one_out[0], two_out[0] = adam_update(master_v[...], one_v[...], two_v[...], grad)

    for copy in (u_pb, u_ma, u_pa, u_mb):
        copy.wait_recv()
    up_out[0] = (upf[0] + up_got[0].astype(F32) + up_got[1].astype(F32)).astype(BF16)

    for sent in started:
        sent.copy.wait_send()


STATE = jax.ShapeDtypeStruct((1, ROWS, HID), F32)
RESULTS = (
    STATE,
    STATE,
    STATE,
    jax.ShapeDtypeStruct((1, TBLK, HID), BF16),
)
SLICES = (FRAGS, 1024)


def run_exchange(*operands):
    vmem = pl.BlockSpec(memory_space=pltpu.VMEM)
    return pl.pallas_call(
        exchange,
        name="exchange",
        out_shape=RESULTS + (jax.ShapeDtypeStruct((QUARTERS,) + SLICES, F32),),
        in_specs=[pl.BlockSpec(memory_space=pl.ANY)] * 6,
        out_specs=(vmem,) * 5,
        scratch_shapes=[
            pltpu.VMEM((2, NX * TBLK, HALF), BF16),
            pltpu.VMEM((COLS, HID), BF16),
            pltpu.VMEM((NX * TBLK, HID), BF16),
            pltpu.VMEM((COLS, HID), F32),
            pltpu.VMEM((3, TBLK, HID), F32),
            pltpu.VMEM((TBLK, HID), BF16),
            pltpu.VMEM((2, TBLK, HID), BF16),
            pltpu.VMEM((2, TBLK // 2, HID), BF16),
            pltpu.VMEM((2, TBLK, HID), BF16),
            pltpu.VMEM((4, ROWS, HID), BF16),
            pltpu.VMEM((4, ROWS, HID), BF16),
            pltpu.VMEM((ROWS, HID), BF16),
            pltpu.VMEM((2, ROWS, HID), BF16),
            pltpu.VMEM((2, ROWS // 2, HID), BF16),
            pltpu.VMEM((2, ROWS, HID), BF16),
            pltpu.VMEM((2,) + SLICES, F32),
            pltpu.VMEM((2,) + SLICES, F32),
            pltpu.VMEM((QUARTERS,) + SLICES, F32),
            pltpu.VMEM((ROWS, HID), F32),
            pltpu.VMEM((ROWS, HID), F32),
            pltpu.VMEM((ROWS, HID), F32),
            pltpu.VMEM((1,) + SLICES, BF16),
            pltpu.SemaphoreType.DMA((N_COPIES,)),
            pltpu.SemaphoreType.DMA((N_COPIES,)),
            pltpu.SemaphoreType.DMA((7,)),
        ],
        compiler_params=pltpu.CompilerParams(
            collective_id=0, has_side_effects=True, vmem_limit_bytes=int(51.85 * 2**20)
        ),
    )(*operands)


def finish(frag_ref, sums, anchor, momentum, master, one, two, up, master_o, one_o, two_o, up_o, anchor_o, momentum_o, buf, sem):
    pairs = ((master, master_o), (one, one_o), (two, two_o), (up, up_o))
    copies = [pltpu.make_async_copy(src, dst, sem.at[i]) for i, (src, dst) in enumerate(pairs)]
    for copy in copies:
        copy.start()
    frag = frag_ref[0]
    for quarter in range(QUARTERS):
        row = slice(quarter, quarter + 1)
        local_sum = sums[quarter, 0:1, :]
        anchor_f = anchor[0, row, :]
        momentum_f = momentum[0, row, :]
        for i in range(1, FRAGS):
            local_sum = jnp.where(frag == i, sums[quarter, i : i + 1, :], local_sum)
            anchor_f = jnp.where(frag == i, anchor[i, row, :], anchor_f)
            momentum_f = jnp.where(frag == i, momentum[i, row, :], momentum_f)
        buf[0, row, :], buf[1, row, :] = nesterov(anchor_f, momentum_f, anchor_f - local_sum * 0.25)
    for i, out in enumerate((anchor_o, momentum_o)):
        copies.append(pltpu.make_async_copy(buf.at[i], out, sem.at[4 + i]))
        copies[-1].start()
    for copy in copies:
        copy.wait()


def run_finish(*given):
    place = pl.BlockSpec(memory_space=pl.ANY)
    vmem = pl.BlockSpec(memory_space=pltpu.VMEM)
    small = jax.ShapeDtypeStruct((QUARTERS, 1024), F32)
    return pl.pallas_call(
        finish,
        name="finish",
        out_shape=RESULTS + (small, small),
        in_specs=[pl.BlockSpec(memory_space=pltpu.SMEM)] + [vmem] * 3 + [place] * 4,
        out_specs=(place,) * 6,
        scratch_shapes=[pltpu.VMEM((2, QUARTERS, 1024), F32), pltpu.SemaphoreType.DMA((6,))],
        compiler_params=pltpu.CompilerParams(vmem_limit_bytes=2**20),
    )(*given)


def local(
    tokens,
    cotangent,
    master,
    moment_one,
    moment_two,
    anchor,
    outer_momentum,
    local_frag,
    frag_index,
):
    *results, sums = run_exchange(tokens, cotangent, master, local_frag, moment_one, moment_two)
    return run_finish(frag_index, sums, anchor, outer_momentum, *results)


def solution(mesh):
    in_specs = (
        P("replica", "fsdp", None),
        P("replica", "fsdp", None),
        P("replica", "fsdp", None),
        P("replica", "fsdp", None),
        P("replica", "fsdp", None),
        P(None, None, "fsdp"),
        P(None, None, "fsdp"),
        P("replica", None, "fsdp"),
        P(),
    )
    out_specs = (
        P("replica", "fsdp", None),
        P("replica", "fsdp", None),
        P("replica", "fsdp", None),
        P("replica", "fsdp", None),
        P(None, "fsdp"),
        P(None, "fsdp"),
    )
    return jax.shard_map(local, mesh=mesh, in_specs=in_specs, out_specs=out_specs, check_vma=False)
```
